32 devices in a mesh: loop: 8 (over z, y), dp: 4 (over x, core).
Axes of the slice: x: 2, y: 2, z: 4, core: 2. Of those that a mesh axis runs over, the one named last changes fastest.
Arguments:
- node_states: bfloat16 [8192, 512], P(('loop', 'dp')), may hold values from -24 to 24
- virtual_states: bfloat16 [64, 512], replicated, may hold values from -6 to 6
- projection: bfloat16 [3, 512, 512], replicated, may hold values from -0.25 to 0.25
- pattern: int32 [64, 5], P(('loop', 'dp')), may hold values from 0 to 63, as said below
- valid_counts: int32 [64], P(('loop', 'dp')), may hold values from 32 to 128, as said below
- node_cotangent: bfloat16 [8192, 512], P(('loop', 'dp')), may hold values from -6 to 6
- virtual_cotangent: bfloat16 [64, 512], replicated, may hold values from -6 to 6
Outputs:
- node_out: bfloat16 [8192, 512], P(('loop', 'dp'))
- virtual_out: bfloat16 [64, 512], replicated
- node_grad: bfloat16 [8192, 512], P(('loop', 'dp'))
- virtual_grad: bfloat16 [64, 512], replicated
- weight_grads: float32 [3, 512, 512], replicated
The draws below stay inside these ranges and needn't reach their ends.
Inputs may be any that keep to these rules, and one draw needn't show every extreme that they name: `pattern`: entry 0 of row b is b. The entries of a row are distinct, and each names a block on the device that holds b or on one of the two devices with the same dp index next to it along the loop axis, which closes (its last index is next to its first). Block b lies on device b // 2, devices numbered with the loop index first. `valid_counts`: at least one block is full.
All inputs are finite; a program needn't handle non-finite values.
Results may differ from the reference program's by a relative error of at most 0.013.
The reference program's roundings to bfloat16 on the way count: a program that leaves them out, or rounds other values in their place, can miss the bound.
Values may be sent and summed in bfloat16 or wider, within the bound.
No kernel may reach another device: no remote copies, remote signals or barrier semaphores. Data moves between devices by JAX's collectives and lax.ppermute only.
A program may use at most 256 MiB of HBM per device.

```python
import jax
import jax.numpy as jnp
from jax import lax

D = 512
H = 8
BLOCK_NODES = 128
VN = 64
KEY_BLOCK_COUNT = 5
BLK_DEV = 2
NBLK = 64
NODES = 8192
N_LOOP = 8
N_DP = 4


def draw_node_states(key, part):
    key = jax.random.fold_in(key, 11)
    return jnp.clip(jax.random.normal(key, (NODES, D), jnp.float32), -6.0, 6.0).astype(jnp.bfloat16)


def draw_pattern(key, part):
    key = jax.random.fold_in(key, 23)
    candidates = 3 * BLK_DEV
    blocks = jnp.arange(NBLK, dtype=jnp.int32)
    device_of = blocks // BLK_DEV
    loop_of = device_of // N_DP
    lane_of = device_of % N_DP
    inner_of = blocks % BLK_DEV
    span = jnp.arange(candidates, dtype=jnp.int32)
    scores = jax.random.randint(key, (NBLK, candidates), 0, 1 << 20, dtype=jnp.int32) * candidates + span[None, :]
    own_index = BLK_DEV + inner_of
    scores = jnp.where(span[None, :] == own_index[:, None], jnp.int32(1 << 30), scores)
    top_scores, picked = lax.top_k(scores, KEY_BLOCK_COUNT)
    picked = picked.astype(jnp.int32)
    circle_offset = picked // BLK_DEV - 1
    target = (loop_of[:, None] + circle_offset + N_LOOP) % N_LOOP * N_DP + lane_of[:, None]
    return (target * BLK_DEV + picked % BLK_DEV).astype(jnp.int32)


def draw_valid_counts(key, part):
    key = jax.random.fold_in(key, 37)
    counts = jax.random.randint(key, (NBLK,), BLOCK_NODES // 4, BLOCK_NODES + 1, dtype=jnp.int32)
    first_pick = jax.random.randint(jax.random.fold_in(key, 1), (), 0, NBLK, dtype=jnp.int32)
    second_pick = (first_pick + 1 + jax.random.randint(jax.random.fold_in(key, 2), (), 0, NBLK - 1, dtype=jnp.int32)) % NBLK
    return counts.at[first_pick].set(BLOCK_NODES).at[second_pick].set(BLOCK_NODES // 4)


def block_levels(key, extent, pieces, low, largest):
    level = 1.0
    for axis_at, shards_of in pieces:
        heights = jax.random.uniform(jax.random.fold_in(jax.random.fold_in(key, 6), axis_at), (shards_of,), jnp.float32, low / len(pieces), largest / len(pieces))
        level = level * jnp.repeat(jnp.exp(heights), extent[axis_at] // shards_of).reshape((-1,) + (1,) * (len(extent) - 1 - axis_at))
    return level


def noise(stream_key, extent, spread, reach, shards=(), held_as=jnp.bfloat16):
    array = spread * jax.random.normal(stream_key, extent, jnp.float32)
    if shards:
        array = array * block_levels(stream_key, extent, shards, -0.22, 0.18)
    return jnp.clip(array, -reach, reach).astype(held_as)


def setup_inputs(seed: int = 0) -> dict:
    seeds = jax.random.split(jax.random.key(seed), 8)
    node_states = draw_node_states(jax.random.fold_in(seeds[7], 71), 0)
    virtual_states = noise(seeds[1], (VN, D), 1.0, 6.0)
    projection = noise(seeds[2], (3, D, D), D ** -0.5, 0.25)
    pattern = draw_pattern(jax.random.fold_in(seeds[7], 71), 0)
    valid_counts = draw_valid_counts(jax.random.fold_in(seeds[7], 71), 0)
    node_cotangent = noise(seeds[5], (NODES, D), 1.0, 6.0, ((0, 32),))
    virtual_cotangent = noise(seeds[6], (VN, D), 1.0, 6.0)
    return {"node_states": node_states, "virtual_states": virtual_states, "projection": projection, "pattern": pattern, "valid_counts": valid_counts, "node_cotangent": node_cotangent, "virtual_cotangent": virtual_cotangent}


NEG_FILL = -1.0e30
HIGHEST = lax.Precision.HIGHEST


def head_split(matrix):
    return matrix.astype(jnp.float32).reshape(matrix.shape[0], H, matrix.shape[1] // H)


def round_bf(values):
    return lax.optimization_barrier(values.astype(jnp.bfloat16)).astype(jnp.float32)


def block_step(query_rows, grad_rows, query_ok, key_rows, value_rows, key_ok):
    score_scale = (D // H) ** -0.5
    query_heads = head_split(query_rows)
    key_heads = head_split(key_rows)
    value_heads = head_split(value_rows)
    raw_scores = jnp.einsum("qhd,khd->hqk", query_heads, key_heads) * score_scale
    raw_scores = jnp.where(key_ok[None, None, :], raw_scores, NEG_FILL)
    row_peak = jnp.max(raw_scores, axis=-1, keepdims=True)
    exponent = jnp.exp(raw_scores - row_peak)
    attention = exponent / jnp.sum(exponent, axis=-1, keepdims=True)
    weights = round_bf(attention)
    mixture = jnp.einsum("hqk,khd->qhd", weights, value_heads).reshape(query_rows.shape)
    node_row_list = jnp.where(query_ok[:, None], mixture, 0.0).astype(jnp.bfloat16)
    masked_grad = jnp.where(query_ok[:, None], grad_rows, jnp.zeros_like(grad_rows))
    grad_heads = head_split(masked_grad)
    weight_grad = jnp.einsum("qhd,khd->hqk", grad_heads, value_heads)
    delta_sum = jnp.sum(attention * weight_grad, axis=-1, keepdims=True)
    score_grad = round_bf(attention * (weight_grad - delta_sum) * score_scale)
    query_gradient = jnp.einsum("hqk,khd->qhd", score_grad, key_heads).reshape(query_rows.shape)
    key_gradient = jnp.einsum("hqk,qhd->khd", score_grad, query_heads).reshape(key_rows.shape)
    value_grad = jnp.einsum("hqk,qhd->khd", weights, grad_heads).reshape(value_rows.shape)
    return node_row_list, query_gradient, key_gradient, value_grad


def reference(node_states, virtual_states, projection, pattern, valid_counts, node_cotangent, virtual_cotangent):
    def project(rows, which):
        return jnp.dot(rows, projection[which], preferred_element_type=jnp.float32).astype(jnp.bfloat16)

    queries = project(node_states, 0)
    keys_all = project(node_states, 1)
    values_all = project(node_states, 2)
    virt_queries = project(virtual_states, 0)
    virt_keys = project(virtual_states, 1)
    virt_values = project(virtual_states, 2)
    positions = jnp.arange(BLOCK_NODES, dtype=jnp.int32)
    block_valid = positions[None, :] < valid_counts[:, None]
    query_blocks = queries.reshape(NBLK, BLOCK_NODES, D)
    key_blocks = keys_all.reshape(NBLK, BLOCK_NODES, D)
    value_blocks = values_all.reshape(NBLK, BLOCK_NODES, D)
    grad_blocks = node_cotangent.reshape(NBLK, BLOCK_NODES, D)

    def scan_step(running_total, block_index):
        key_sum_total, value_sum_total, virtual_key_total, virtual_value_total = running_total
        chosen = pattern[block_index]
        key_rows = jnp.concatenate([key_blocks[chosen].reshape(KEY_BLOCK_COUNT * BLOCK_NODES, D), virt_keys], axis=0)
        value_rows = jnp.concatenate([value_blocks[chosen].reshape(KEY_BLOCK_COUNT * BLOCK_NODES, D), virt_values], axis=0)
        key_ok = jnp.concatenate([block_valid[chosen].reshape(KEY_BLOCK_COUNT * BLOCK_NODES), jnp.ones((VN,), dtype=jnp.bool_)])
        node_row_list, query_gradient, key_gradient, value_grad = block_step(
            query_blocks[block_index], grad_blocks[block_index], block_valid[block_index], key_rows, value_rows, key_ok)
        key_sum_total = key_sum_total.at[chosen].add(key_gradient[: KEY_BLOCK_COUNT * BLOCK_NODES].reshape(KEY_BLOCK_COUNT, BLOCK_NODES, D))
        value_sum_total = value_sum_total.at[chosen].add(value_grad[: KEY_BLOCK_COUNT * BLOCK_NODES].reshape(KEY_BLOCK_COUNT, BLOCK_NODES, D))
        virtual_key_total = virtual_key_total + key_gradient[KEY_BLOCK_COUNT * BLOCK_NODES:]
        virtual_value_total = virtual_value_total + value_grad[KEY_BLOCK_COUNT * BLOCK_NODES:]
        return (key_sum_total, value_sum_total, virtual_key_total, virtual_value_total), (node_row_list, query_gradient)

    initial = (jnp.zeros((NBLK, BLOCK_NODES, D), jnp.float32), jnp.zeros((NBLK, BLOCK_NODES, D), jnp.float32),
               jnp.zeros((VN, D), jnp.float32), jnp.zeros((VN, D), jnp.float32))
    running_total, stacked = lax.scan(scan_step, initial, jnp.arange(NBLK, dtype=jnp.int32))
    key_sum_total, value_sum_total, virtual_key_total, virtual_value_total = running_total
    node_out = stacked[0].reshape(NODES, D)
    query_gradient = stacked[1].reshape(NODES, D)

    score_scale = (D // H) ** -0.5
    node_ok = block_valid.reshape(NODES)
    key_heads = head_split(keys_all)
    value_heads = head_split(values_all)
    virt_query_heads = head_split(virt_queries)
    virt_scores = jnp.einsum("uhd,nhd->hun", virt_query_heads, key_heads) * score_scale
    virt_scores = jnp.where(node_ok[None, None, :], virt_scores, NEG_FILL)
    virt_peak = jnp.max(virt_scores, axis=-1, keepdims=True)
    virt_exp = jnp.exp(virt_scores - virt_peak)
    virt_total = jnp.sum(virt_exp, axis=-1, keepdims=True)
    virt_mixed = jnp.einsum("hun,nhd->hud", virt_exp, value_heads, precision=HIGHEST) / virt_total
    virtual_out = jnp.transpose(virt_mixed, (1, 0, 2)).reshape(VN, D).astype(jnp.bfloat16)
    virt_attn = virt_exp / virt_total
    virt_grad_heads = head_split(virtual_cotangent)
    virt_dw = jnp.einsum("uhd,nhd->hun", virt_grad_heads, value_heads)
    virt_delta = jnp.sum(virt_grad_heads * jnp.transpose(virt_mixed, (1, 0, 2)), axis=-1).T
    virt_ds = round_bf(virt_attn * (virt_dw - virt_delta[..., None]) * score_scale)
    virtual_query_gradient = jnp.einsum("hun,nhd->uhd", virt_ds, key_heads).reshape(VN, D)
    key_node = key_sum_total.reshape(NODES, D) + jnp.einsum("hun,uhd->nhd", virt_ds, virt_query_heads).reshape(NODES, D)
    value_node = value_sum_total.reshape(NODES, D) + jnp.einsum("hun,uhd->nhd", round_bf(virt_attn), virt_grad_heads).reshape(NODES, D)

    grads = [query_gradient.astype(jnp.bfloat16), key_node.astype(jnp.bfloat16), value_node.astype(jnp.bfloat16)]
    virtual_gradients = [virtual_query_gradient, virtual_key_total, virtual_value_total]
    node_grad = jnp.zeros((NODES, D), jnp.float32)
    virtual_grad = jnp.zeros((VN, D), jnp.float32)
    weight_list = []
    for which in range(3):
        node_grad = node_grad + jnp.dot(grads[which], projection[which].T, preferred_element_type=jnp.float32)
        virtual_grad = virtual_grad + jnp.dot(virtual_gradients[which], projection[which].astype(jnp.float32).T, precision=HIGHEST)
        weight_list.append(jnp.dot(node_states.T, grads[which], preferred_element_type=jnp.float32)
                           + jnp.dot(virtual_states.astype(jnp.float32).T, virtual_gradients[which], precision=HIGHEST))
    weight_grads = jnp.stack(weight_list)
    return node_out, virtual_out, node_grad.astype(jnp.bfloat16), virtual_grad.astype(jnp.bfloat16), weight_grads
```

```python
import functools

import jax
import jax.numpy as jnp
from jax import lax
from jax.experimental import pallas as pl
from jax.experimental.pallas import tpu as pltpu
from jax.sharding import PartitionSpec as P

H = 8
NEG_FILL = -1e30
SHARDS = 32
BF = jnp.bfloat16
F32 = jnp.float32


def nn(a, b):
    return lax.dot_general(a, b, (((1,), (0,)), ((), ())), preferred_element_type=F32)


def nt(a, b):
    return lax.dot_general(a, b, (((1,), (1,)), ((), ())), preferred_element_type=F32)


def tn(a, b):
    return lax.dot_general(a, b, (((0,), (0,)), ((), ())), preferred_element_type=F32)


def lane_half(pair, half):
    lane = lax.broadcasted_iota(jnp.int32, pair.shape, 1)
    width = pair.shape[1] // 2
    keep = lane < width if half == 0 else lane >= width
    return jnp.where(keep, pair, jnp.zeros_like(pair))


def both_heads(pair):
    return jnp.concatenate([lane_half(pair, 0), lane_half(pair, 1)], axis=0)


def own_row_ok(counts_ref, blocks, block_rows, shape):
    row = lax.broadcasted_iota(jnp.int32, shape, 0)
    limit = jnp.full(shape, counts_ref[0], jnp.int32)
    for b in range(1, blocks):
        limit = jnp.where(row < b * block_rows, limit, b * block_rows + counts_ref[b])
    return row < limit


def project_kernel(blocks, block_rows, score_scale, counts_ref, x_ref, vs_ref, vcot_ref, w_ref,
                   q_ref, k_ref, v_ref, virt_ref, stats_ref):
    x = x_ref[...]
    k = nn(x, w_ref[1]).astype(BF)
    v = nn(x, w_ref[2]).astype(BF)
    k_ref[...] = k
    v_ref[...] = v
    virt = [nn(vs_ref[...], w_ref[t]).astype(BF) for t in range(3)]
    for t in range(3):
        virt_ref[t] = virt[t]
    virt_q = virt[0] * score_scale
    n, width = x.shape
    ok = own_row_ok(counts_ref, blocks, block_rows, (n, 128))
    peaks, totals, deltas = [], [], []
    for c in range(0, width, 128):
        scores = nt(k[:, c:c + 128], both_heads(virt_q[:, c:c + 128]))
        scores = jnp.where(ok, scores, NEG_FILL)
        peak = jnp.max(scores, axis=0, keepdims=True)
        e = jnp.where(ok, jnp.exp(scores - peak), 0.0)
        dw = nt(v[:, c:c + 128], both_heads(vcot_ref[:, c:c + 128]))
        peaks.append(peak)
        totals.append(jnp.sum(e, axis=0, keepdims=True))
        deltas.append(jnp.sum(e * dw, axis=0, keepdims=True))
    rows = jnp.concatenate(peaks + totals + deltas + peaks, axis=0)
    stats_ref[...] = jnp.broadcast_to(rows[None], stats_ref.shape)
    q_ref[...] = nn(x, w_ref[0]).astype(BF) * score_scale


def attention_kernel(blocks, block_rows, lanes, score_scale, place_ref, pat_ref, cl_ref, co_ref, cr_ref, xl_ref, xr_ref,
                     w_ref, q_ref, k_ref, v_ref, g_ref, virt_ref, out_ref, dq_ref, dk_ref, dv_ref,
                     key_s, val_s, bias_s, ot_s, dqt_s):
    n, width = q_ref.shape
    virtual_rows = virt_ref.shape[1]
    loop_here, loop_size = place_ref[0], place_ref[1]
    for at, ref in ((0, xl_ref), (2, xr_ref)):
        x = ref[...]
        key_s[at * n:(at + 1) * n, :] = nn(x, w_ref[1]).astype(BF)
        val_s[at * n:(at + 1) * n, :] = nn(x, w_ref[2]).astype(BF)
    key_s[n:2 * n, :] = k_ref[...]
    val_s[n:2 * n, :] = v_ref[...]
    key_s[3 * n:3 * n + virtual_rows, :] = virt_ref[1]
    val_s[3 * n:3 * n + virtual_rows, :] = virt_ref[2]
    row = lax.broadcasted_iota(jnp.int32, (block_rows, block_rows), 0)
    for i in range(blocks):
        slots = []
        for j in range(pat_ref.shape[1]):
            block = pat_ref[i, j]
            ring = (block // blocks) // lanes
            offset = lax.rem(ring - loop_here + 1 + 2 * loop_size, loop_size)
            slots.append(offset * blocks + lax.rem(block, blocks))
        for b in range(3 * blocks):
            count = (cl_ref, co_ref, cr_ref)[b // blocks][b % blocks]
            listed = slots[0] == b
            for s in slots[1:]:
                listed = jnp.logical_or(listed, s == b)
            count = jnp.where(listed, count, 0)
            bias_s[b * block_rows:(b + 1) * block_rows, i * block_rows:(i + 1) * block_rows] = jnp.where(
                row < count, 0.0, NEG_FILL)
    bias_s[3 * n:3 * n + virtual_rows, :] = jnp.zeros((virtual_rows, n), F32)
    ok = own_row_ok(co_ref, blocks, block_rows, (n, 128))
    for c in range(0, width, 128):
        k_pair, v_pair = key_s[:, c:c + 128], val_s[:, c:c + 128]
        q_pair = q_ref[:, c:c + 128]
        g_pair = jnp.where(ok, g_ref[:, c:c + 128], jnp.zeros((n, 128), BF))
        dk_pair = dv_pair = None
        for half in range(2):
            qm, gm = lane_half(q_pair, half), lane_half(g_pair, half)
            s = nt(k_pair, qm) + bias_s[...]
            e = jnp.exp(s - jnp.max(s, axis=0, keepdims=True))
            a = e * (1.0 / jnp.sum(e, axis=0, keepdims=True))
            wt = a.astype(BF)
            dw = nt(v_pair, gm)
            delta = jnp.sum(a * dw, axis=0, keepdims=True)
            ds = (a * (dw - delta)).astype(BF)
            at = c + half * 64
            ot_s[at:at + 64, :] = tn(v_pair, wt)[half * 64:half * 64 + 64]
            dqt_s[at:at + 64, :] = tn(k_pair, ds)[half * 64:half * 64 + 64]
            dk, dv = nn(ds, qm), nn(wt, gm)
            dk_pair = dk if dk_pair is None else dk_pair + dk
            dv_pair = dv if dv_pair is None else dv_pair + dv
        dk_ref[:, c:c + 128] = dk_pair
        dv_ref[:, c:c + 128] = dv_pair
    okw = own_row_ok(co_ref, blocks, block_rows, (n, width))
    out_ref[...] = jnp.where(okw, ot_s[...].T, 0.0).astype(BF)
    dq_ref[...] = (dqt_s[...].T * score_scale).astype(BF)


def weight_kernel(blocks, block_rows, score_scale, counts_ref, ids_ref, x_ref, xl_ref, xr_ref, vs_ref, vcot_ref, w_ref,
                  k_ref, v_ref, virt_ref, stats_ref, dq_ref, dk_ref, dv_ref,
                  keep_a, send_a, keep_b, send_b, kown_ref, vown_ref, wg_s, vg_s, vo_s, vgrad_s, dkw_s, dvw_s):
    n, width = x_ref.shape
    virtual_rows = vs_ref.shape[0]
    ok = own_row_ok(counts_ref, blocks, block_rows, (n, 128))
    pairs = width // 128
    stats = stats_ref[...]
    peak = jnp.max(stats[:, 0:pairs], axis=0)
    factor = jnp.exp(stats[:, 0:pairs] - peak[None])
    total = jnp.sum(stats[:, pairs:2 * pairs] * factor, axis=0)
    delta = jnp.sum(stats[:, 2 * pairs:3 * pairs] * factor, axis=0) / total
    inv_total = 1.0 / total
    lane_low = lax.broadcasted_iota(jnp.int32, (virtual_rows, 128), 1) < 64

    def diagonal(square):
        return jnp.where(lane_low, square[:virtual_rows], square[virtual_rows:])

    dkw_s[...] = dk_ref[0:3 * n, :].astype(BF)
    dvw_s[...] = dv_ref[0:3 * n, :].astype(BF)
    for p in range(pairs):
        c = p * 128
        k_pair, v_pair = k_ref[:, c:c + 128], v_ref[:, c:c + 128]
        vq = both_heads(virt_ref[0, :, c:c + 128])
        vcot = both_heads(vcot_ref[:, c:c + 128])
        scores = jnp.where(ok, nt(k_pair, vq * score_scale), NEG_FILL)
        attn = jnp.exp(scores - peak[p:p + 1]) * inv_total[p:p + 1]
        attn_hi = attn.astype(BF)
        attn_lo = (attn - attn_hi.astype(F32)).astype(BF)
        dw = nt(v_pair, vcot)
        ds = (attn * (dw - delta[p:p + 1]) * score_scale).astype(BF)
        vo_s[:, c:c + 128] = diagonal(tn(attn_hi, v_pair) + tn(attn_lo, v_pair))
        vgrad_s[0, :, c:c + 128] = diagonal(tn(ds, k_pair))
        dkw_s[n:2 * n, c:c + 128] = (dk_ref[n:2 * n, c:c + 128] + nn(ds, vq)).astype(BF)
        dvw_s[n:2 * n, c:c + 128] = (dv_ref[n:2 * n, c:c + 128] + nn(attn_hi, vcot)).astype(BF)
    vgrad_s[1] = dk_ref[3 * n:3 * n + virtual_rows, :]
    vgrad_s[2] = dv_ref[3 * n:3 * n + virtual_rows, :]
    xs = jnp.concatenate([xl_ref[...], x_ref[...], xr_ref[...]], axis=0)
    vs = vs_ref[...]
    vg = None
    for t in range(3):
        part = vgrad_s[t]
        hi = part.astype(BF)
        lo = (part - hi.astype(F32)).astype(BF)
        if t == 0:
            wg = tn(x_ref[...], dq_ref[...])
        else:
            wg = tn(xs, (dkw_s if t == 1 else dvw_s)[...])
        wg_s[t] = wg + (tn(vs, hi) + tn(vs, lo))
        back = nt(hi, w_ref[t]) + nt(lo, w_ref[t])
        vg = back if vg is None else vg + back
    vg_s[...] = vg
    row_groups = width // 64
    for name, refs in ((0, (keep_a, send_a)), (1, (keep_b, send_b))):
        me = ids_ref[name]
        for p in range(SHARDS):
            ref, at = refs[p // (SHARDS // 2)], p % (SHARDS // 2)
            shard = jnp.bitwise_xor(me, p)
            cols = pl.ds(pl.multiple_of((shard // row_groups) * 128, 128), 128)
            group = lax.rem(shard, row_groups)
            for t in range(3):
                rows = pl.ds(pl.multiple_of(group * 64 + name * 32, 32), 32)
                ref[at, t * 32:(t + 1) * 32, :] = wg_s[t, rows, cols].astype(BF)
            if name == 0:
                rows = pl.ds(pl.multiple_of(group * 8, 8), 8)
                ref[at, 96:112, :] = jnp.concatenate([vg_s[rows, cols], vo_s[rows, cols]], axis=0).astype(BF)
    kown_ref[...] = dkw_s[...]
    vown_ref[...] = dvw_s[...]


def node_kernel(w_ref, dq_ref, dk_ref, dv_ref, left_ref, right_ref, own_ref):
    n = dq_ref.shape[0]
    for at, ref in ((0, left_ref), (2, right_ref), (1, own_ref)):
        rows = slice(at * n, (at + 1) * n)
        part = nt(dk_ref[rows, :], w_ref[1]) + nt(dv_ref[rows, :], w_ref[2])
        if at == 1:
            part = part + nt(dq_ref[...], w_ref[0])
        ref[...] = part.astype(ref.dtype)


def unpack_kernel(ids_ref, a0_ref, a1_ref, b0_ref, b1_ref, wg_ref, vg_ref, vo_ref):
    width = wg_ref.shape[2]
    row_groups = width // 64
    for name, refs in ((0, (a0_ref, a1_ref)), (1, (b0_ref, b1_ref))):
        me = ids_ref[name]
        for p in range(SHARDS):
            ref, at = refs[p // (SHARDS // 2)], p % (SHARDS // 2)
            shard = jnp.bitwise_xor(me, p)
            cols = pl.ds(pl.multiple_of((shard // row_groups) * 128, 128), 128)
            group = lax.rem(shard, row_groups)
            for t in range(3):
                rows = pl.ds(pl.multiple_of(group * 64 + name * 32, 32), 32)
                wg_ref[t, rows, cols] = ref[at, t * 32:(t + 1) * 32, :].astype(F32)
            if name == 0:
                rows = pl.ds(pl.multiple_of(group * 8, 8), 8)
                both = ref[at, 96:112, :].astype(F32)
                vg_ref[rows, cols] = both[0:8]
                vo_ref[rows, cols] = both[8:16]


SMEM = pl.BlockSpec(memory_space=pltpu.SMEM)
VMEM = pl.BlockSpec(memory_space=pltpu.VMEM)


def call(body, args, specs, outs, scratch=(), flops=1e8, name=None):
    return pl.pallas_call(
        body,
        out_shape=[jax.ShapeDtypeStruct(s, d) for s, d in outs],
        in_specs=specs,
        out_specs=[VMEM] * len(outs),
        scratch_shapes=[pltpu.VMEM(s, d) for s, d in scratch],
        compiler_params=pltpu.CompilerParams(vmem_limit_bytes=40 << 20),
        cost_estimate=pl.CostEstimate(flops=int(flops), bytes_accessed=4 << 20, transcendentals=0),
        name=name,
    )(*args)


def ring(value, steps):
    count = lax.axis_size("loop")
    return lax.ppermute(value, "loop", [(s, (s + steps) % count) for s in range(count)])


def swap(value, axis, bit):
    return lax.ppermute(value, axis, [(s, s ^ bit) for s in range(lax.axis_size(axis))])


def add(a, b):
    return (a.astype(F32) + b.astype(F32)).astype(BF)


def reduce_all(keep_a, send_a, keep_b, send_b):
    loop_size = lax.axis_size("loop")
    x_bit, y_bit = ("dp", 2), ("loop", 1)
    orders = {"a": (x_bit, y_bit), "b": (y_bit, x_bit)}
    held = {"a": add(keep_a, swap(send_a, "dp", 1)), "b": add(keep_b, swap(send_b, "dp", 1))}
    for step in range(2):
        halves = {k: h.shape[0] // 2 for k, h in held.items()}
        got = {k: swap(h[halves[k]:], *orders[k][step]) for k, h in held.items()}
        held = {k: add(h[:halves[k]], got[k]) for k, h in held.items()}
    both = jnp.concatenate([held["a"], held["b"]], axis=1)
    got = [swap(both[j], "loop", 2 * j) for j in range(1, 4)]
    piece = both[0].astype(F32)
    for g in got:
        piece = piece + g.astype(F32)
    piece = piece.astype(BF)
    bit = 8
    while bit < loop_size:
        piece = add(piece, swap(piece, "loop", bit))
        bit *= 2
    full = jnp.stack([piece] + [swap(piece, "loop", 2 * j) for j in range(1, 4)])
    rows_a = keep_a.shape[1]
    held = {"a": full[:, :rows_a], "b": full[:, rows_a:]}
    for step in (1, 0):
        got = {k: swap(h, *orders[k][step]) for k, h in held.items()}
        held = {k: jnp.concatenate([h, got[k]], axis=0) for k, h in held.items()}
    return held["a"], swap(held["a"], "dp", 1), held["b"], swap(held["b"], "dp", 1)


def local(node_states, virtual_states, projection, pattern, valid_counts, node_cotangent, virtual_cotangent):
    n, width = node_states.shape
    blocks = pattern.shape[0]
    block_rows = n // blocks
    virtual_rows = virtual_states.shape[0]
    loop_size, lanes = lax.axis_size("loop"), lax.axis_size("dp")
    devices = loop_size * lanes
    loop_here, lane_here = lax.axis_index("loop"), lax.axis_index("dp")
    score_scale = (width // H) ** -0.5
    keys = 3 * n + virtual_rows

    x_left, x_right = ring(node_states, 1), ring(node_states, -1)
    c_left, c_right = ring(valid_counts, 1), ring(valid_counts, -1)

    place = jnp.stack([loop_here, jnp.int32(loop_size)]).astype(jnp.int32)
    core, x_at = lane_here & 1, (lane_here >> 1) & 1
    y_at, z_at = loop_here & 1, (loop_here >> 1) & 3
    ids = jnp.stack([core * 16 + x_at * 8 + y_at * 4 + z_at, core * 16 + y_at * 8 + x_at * 4 + z_at]).astype(jnp.int32)

    q, k, v, virt, stats = call(
        functools.partial(project_kernel, blocks, block_rows, score_scale),
        (valid_counts, node_states, virtual_states, virtual_cotangent, projection),
        [SMEM] + [VMEM] * 4,
        [((n, width), BF)] * 3 + [((3, virtual_rows, width), BF), ((devices, 16, 128), F32)],
        name="project")
    stats = lax.all_to_all(stats, ("loop", "dp"), 0, 0, tiled=True)

    node_out, dq, dk, dv = call(
        functools.partial(attention_kernel, blocks, block_rows, lanes, score_scale),
        (place, pattern, c_left, valid_counts, c_right, x_left, x_right, projection, q, k, v, node_cotangent, virt),
        [SMEM] * 5 + [VMEM] * 8,
        [((n, width), BF)] * 2 + [((keys, width), F32)] * 2,
        [((keys, width), BF)] * 2 + [((keys, n), F32)] + [((width, n), F32)] * 2,
        flops=4e9, name="attention")

    keep_a, send_a, keep_b, send_b, dk_all, dv_all = call(
        functools.partial(weight_kernel, blocks, block_rows, score_scale),
        (valid_counts, ids, node_states, x_left, x_right, virtual_states, virtual_cotangent, projection, k, v, virt, stats,
         dq, dk, dv),
        [SMEM] * 2 + [VMEM] * 13,
        [((SHARDS // 2, 112, 128), BF)] * 2 + [((SHARDS // 2, 96, 128), BF)] * 2 + [((3 * n, width), BF)] * 2,
        [((3, width, width), F32)] + [((virtual_rows, width), F32)] * 2 + [((3, virtual_rows, width), F32)]
        + [((3 * n, width), BF)] * 2,
        flops=1.2e9, name="weight_grads")

    to_left, to_right, own_part = call(
        node_kernel, (projection, dq, dk_all, dv_all), [VMEM] * 4,
        [((n, width), BF)] * 2 + [((n, width), F32)], flops=1e9, name="node_grads")
    from_right, from_left = ring(to_left, -1), ring(to_right, 1)

    pieces = reduce_all(keep_a, send_a, keep_b, send_b)
    node_grad = (own_part + from_right.astype(F32) + from_left.astype(F32)).astype(BF)
    weight_grads, virtual_grad, virtual_out = call(
        unpack_kernel, (ids,) + tuple(pieces), [SMEM] + [VMEM] * 4,
        [((3, width, width), F32)] + [((virtual_rows, width), F32)] * 2, name="unpack")
    return node_out, virtual_out.astype(BF), node_grad, virtual_grad.astype(BF), weight_grads


def solution(mesh):
    return jax.shard_map(
        local,
        mesh=mesh,
        in_specs=(
            P(("loop", "dp"), None),
            P(),
            P(),
            P(("loop", "dp"), None),
            P(("loop", "dp")),
            P(("loop", "dp"), None),
            P(),
        ),
        out_specs=(P(("loop", "dp"), None), P(), P(("loop", "dp"), None), P(), P()),
        check_vma=False,
    )
```

```python
import functools

import jax
import jax.numpy as jnp
from jax import lax
from jax.experimental import pallas as pl
from jax.experimental.pallas import tpu as pltpu
from jax.sharding import PartitionSpec as P

H = 8
NEG_FILL = -1e30
SHARDS = 32
ABSENT = 1000.0
VMEM_BYTES = 60 << 20
BF = jnp.bfloat16
F32 = jnp.float32


def nn(a, b):
    return lax.dot_general(a, b, (((1,), (0,)), ((), ())), preferred_element_type=F32)


def nt(a, b):
    return lax.dot_general(a, b, (((1,), (1,)), ((), ())), preferred_element_type=F32)


def tn(a, b):
    return lax.dot_general(a, b, (((0,), (0,)), ((), ())), preferred_element_type=F32)


def lane_half(pair, half):
    lane = lax.broadcasted_iota(jnp.int32, pair.shape, 1)
    width = pair.shape[1] // 2
    keep = lane < width if half == 0 else lane >= width
    return jnp.where(keep, pair, jnp.zeros_like(pair))


def both_heads(pair):
    return jnp.concatenate([lane_half(pair, 0), lane_half(pair, 1)], axis=0)


def own_row_ok(counts_ref, blocks, block_rows, shape):
    row = lax.broadcasted_iota(jnp.int32, shape, 0)
    limit = jnp.full(shape, counts_ref[0], jnp.int32)
    for b in range(1, blocks):
        limit = jnp.where(row < b * block_rows, limit, b * block_rows + counts_ref[b])
    return row < limit


def loader(srcs, dsts, sems):
    copies = [pltpu.make_async_copy(src, dst, sems.at[i]) for i, (src, dst) in enumerate(zip(srcs, dsts))]
    for copy in copies:
        copy.start()

    def ready(*which):
        for i in which:
            copies[i].wait()

    return ready


class Writer:
    def __init__(self, sems, base):
        self.sems, self.base, self.copies = sems, base, []

    def send(self, src, dst):
        copy = pltpu.make_async_copy(src, dst, self.sems.at[self.base + len(self.copies)])
        copy.start()
        self.copies.append(copy)

    def finish(self):
        for copy in self.copies:
            copy.wait()


def place():
    loop_here, lane_here = lax.axis_index("loop"), lax.axis_index("dp")
    core, x_at = lane_here & 1, (lane_here >> 1) & 1
    y_at, z_at = loop_here & 1, (loop_here >> 1) & 3
    return core * 16 + x_at * 8 + y_at * 4 + z_at


def project_kernel(blocks, block_rows, score_scale, counts_h, x_h, w_h, vs_h, vcot_h,
                   q_h, k_h, v_h, virt_h, stats_h, x_ref, w_ref, vs_ref, vcot_ref, q_s, k_s, v_s, virt_s, stats_s, counts_ref, sems):
    ready = loader((x_h, w_h.at[1], w_h.at[2], vs_h, w_h.at[0], vcot_h, counts_h),
                   (x_ref, w_ref.at[1], w_ref.at[2], vs_ref, w_ref.at[0], vcot_ref, counts_ref), sems)
    out = Writer(sems, 7)
    ready(0, 1, 2)
    x = x_ref[...]
    k = nn(x, w_ref[1]).astype(BF)
    v = nn(x, w_ref[2]).astype(BF)
    k_s[...] = k
    v_s[...] = v
    out.send(k_s, k_h)
    out.send(v_s, v_h)
    ready(3, 4, 5, 6)
    virt_q = nn(vs_ref[...], w_ref[0]).astype(BF)
    virt_s[0] = virt_q
    virt_s[1] = nn(vs_ref[...], w_ref[1]).astype(BF)
    virt_s[2] = nn(vs_ref[...], w_ref[2]).astype(BF)
    out.send(virt_s, virt_h)
    virt_q = virt_q * score_scale
    n, width = x.shape
    ok = own_row_ok(counts_ref, blocks, block_rows, (n, 128))
    peaks, totals, deltas = [], [], []
    for c in range(0, width, 128):
        scores = nt(k[:, c:c + 128], both_heads(virt_q[:, c:c + 128]))
        scores = jnp.where(ok, scores, NEG_FILL)
        peak = jnp.max(scores, axis=0, keepdims=True)
        e = jnp.where(ok, jnp.exp(scores - peak), 0.0)
        dw = nt(v[:, c:c + 128], both_heads(vcot_ref[:, c:c + 128]))
        peaks.append(peak)
        totals.append(jnp.sum(e, axis=0, keepdims=True))
        deltas.append(jnp.sum(e * dw, axis=0, keepdims=True))
    rows = jnp.concatenate(peaks + totals + deltas + peaks, axis=0)
    stats_s[...] = jnp.broadcast_to(rows[None], stats_s.shape)
    out.send(stats_s, stats_h)
    q_s[...] = nn(x, w_ref[0]).astype(BF) * score_scale
    out.send(q_s, q_h)
    out.finish()


def attention_kernel(blocks, block_rows, score_scale, pat_h, co_h, xl_h, xr_h,
                     w_h, q_h, k_h, v_h, g_h, virt_h,
                     out_h, dq_h, left_h, right_h, dkn_h, dvn_h, dko_h, dvo_h,
                     xl_ref, xr_ref, w_ref, q_ref, g_ref,
                     key_s, val_s, bias_s, ot_s, dqt_s, out_s, dq_s, dkn_s, dvn_s, dko_s, dvo_s, left_s, right_s, pat_ref, co_ref, sems):
    n, width = q_ref.shape
    virtual_rows = virt_h.shape[1]
    loop_here, loop_size, lanes = lax.axis_index("loop"), lax.axis_size("loop"), lax.axis_size("dp")
    own, virt = pl.ds(n, n), pl.ds(3 * n, virtual_rows)
    ready = loader((xl_h, xr_h, w_h.at[1], w_h.at[2], k_h, v_h, virt_h.at[1], virt_h.at[2], q_h, g_h, pat_h, co_h),
                   (xl_ref, xr_ref, w_ref.at[0], w_ref.at[1], key_s.at[own], val_s.at[own],
                    key_s.at[virt], val_s.at[virt], q_ref, g_ref, pat_ref, co_ref), sems)
    out = Writer(sems, 12)
    row = lax.broadcasted_iota(jnp.int32, (block_rows, block_rows), 0)
    bias_s[3 * n:3 * n + virtual_rows, :] = jnp.zeros((virtual_rows, n), F32)
    ready(0, 1, 10, 11)
    for i in range(blocks):
        slots = []
        for j in range(pat_ref.shape[1]):
            block = pat_ref[i, j]
            ring_at = (block // blocks) // lanes
            offset = lax.rem(ring_at - loop_here + 1 + 2 * loop_size, loop_size)
            slots.append(offset * blocks + lax.rem(block, blocks))
        for b in range(3 * blocks):
            listed = slots[0] == b
            for s in slots[1:]:
                listed = jnp.logical_or(listed, s == b)
            at, inner = b // blocks, b % blocks
            if at == 1:
                okb = row < jnp.where(listed, co_ref[inner], 0)
            else:
                x_ref = (xl_ref, None, xr_ref)[at]
                mark = x_ref[inner * block_rows:(inner + 1) * block_rows, 0:128].astype(F32)[:, 0:1]
                okb = jnp.broadcast_to(mark, (block_rows, block_rows)) < jnp.where(listed, 0.5 * ABSENT, -ABSENT)
            bias_s[b * block_rows:(b + 1) * block_rows, i * block_rows:(i + 1) * block_rows] = jnp.where(
                okb, 0.0, NEG_FILL)
    ready(2, 3)
    for at, ref in ((0, xl_ref), (2, xr_ref)):
        x = ref[...]
        key_s[at * n:(at + 1) * n, :] = nn(x, w_ref[0]).astype(BF)
        val_s[at * n:(at + 1) * n, :] = nn(x, w_ref[1]).astype(BF)
    ready(4, 5, 6, 7, 8, 9)
    ok = own_row_ok(co_ref, blocks, block_rows, (n, 128))
    for c in range(0, width, 128):
        k_pair, v_pair = key_s[:, c:c + 128], val_s[:, c:c + 128]
        q_pair = q_ref[:, c:c + 128]
        g_pair = jnp.where(ok, g_ref[:, c:c + 128], jnp.zeros((n, 128), BF))
        dk_pair = dv_pair = None
        for half in range(2):
            qm, gm = lane_half(q_pair, half), lane_half(g_pair, half)
            s = nt(k_pair, qm) + bias_s[...]
            e = jnp.exp(s - jnp.max(s, axis=0, keepdims=True))
            a = e * (1.0 / jnp.sum(e, axis=0, keepdims=True))
            wt = a.astype(BF)
            dw = nt(v_pair, gm)
            delta = jnp.sum(a * dw, axis=0, keepdims=True)
            ds = (a * (dw - delta)).astype(BF)
            at = c + half * 64
            ot_s[at:at + 64, :] = tn(v_pair, wt)[half * 64:half * 64 + 64]
            dqt_s[at:at + 64, :] = tn(k_pair, ds)[half * 64:half * 64 + 64]
            dk, dv = nn(ds, qm), nn(wt, gm)
            dk_pair = dk if dk_pair is None else dk_pair + dk
            dv_pair = dv if dv_pair is None else dv_pair + dv
        for near, mine, part in ((dkn_s, dko_s, dk_pair), (dvn_s, dvo_s, dv_pair)):
            near[0:n, c:c + 128] = part[0:n].astype(BF)
            near[n:2 * n, c:c + 128] = part[2 * n:3 * n].astype(BF)
            mine[0:n, c:c + 128] = part[n:2 * n]
            mine[n:n + virtual_rows, c:c + 128] = part[3 * n:3 * n + virtual_rows]
    for rows, ref, dst in ((slice(0, n), left_s, left_h), (slice(n, 2 * n), right_s, right_h)):
        ref[...] = (nt(dkn_s[rows, :], w_ref[0]) + nt(dvn_s[rows, :], w_ref[1])).astype(BF)
        out.send(ref, dst)
    out.send(dkn_s, dkn_h)
    out.send(dvn_s, dvn_h)
    out.send(dko_s, dko_h)
    out.send(dvo_s, dvo_h)
    dq_s[...] = (dqt_s[...].T * score_scale).astype(BF)
    out.send(dq_s, dq_h)
    okw = own_row_ok(co_ref, blocks, block_rows, (n, width))
    out_s[...] = jnp.where(okw, ot_s[...].T, 0.0).astype(BF)
    out.send(out_s, out_h)
    out.finish()


def weight_kernel(blocks, block_rows, score_scale, counts_h, x_h, xl_h, xr_h, vs_h, vcot_h, w_h,
                  k_h, v_h, virt_h, stats_h, dq_h, dkn_h, dvn_h, dko_h, dvo_h,
                  keep_h, send_h, kown_h, vown_h,
                  xs_ref, vs_ref, vcot_ref, w_ref, k_ref, v_ref, virt_ref, stats_ref, dq_ref, dk_ref, dv_ref,
                  keep_s, send_s, wg_s, vg_s, vo_s, vgrad_s, dkw_s, dvw_s, counts_ref, sems):
    n, width = x_h.shape
    virtual_rows = vs_ref.shape[0]
    low, own, high = pl.ds(0, n), pl.ds(n, n), pl.ds(2 * n, n)
    ready = loader((stats_h, k_h, v_h, virt_h.at[0], vcot_h, dko_h, dvo_h, dq_h,
                    x_h, xl_h, xr_h, vs_h, w_h, counts_h, dkn_h.at[low], dkn_h.at[own], dvn_h.at[low], dvn_h.at[own]),
                   (stats_ref, k_ref, v_ref, virt_ref, vcot_ref, dk_ref, dv_ref, dq_ref,
                    xs_ref.at[own], xs_ref.at[low], xs_ref.at[high], vs_ref, w_ref, counts_ref,
                    dkw_s.at[low], dkw_s.at[high], dvw_s.at[low], dvw_s.at[high]), sems)
    out = Writer(sems, 18)
    pairs = width // 128
    ready(0, 13)
    ok = own_row_ok(counts_ref, blocks, block_rows, (n, 128))
    stats = stats_ref[...]
    peak = jnp.max(stats[:, 0:pairs], axis=0)
    factor = jnp.exp(stats[:, 0:pairs] - peak[None])
    total = jnp.sum(stats[:, pairs:2 * pairs] * factor, axis=0)
    delta = jnp.sum(stats[:, 2 * pairs:3 * pairs] * factor, axis=0) / total
    inv_total = 1.0 / total
    lane_low = lax.broadcasted_iota(jnp.int32, (virtual_rows, 128), 1) < 64

    def diagonal(square):
        return jnp.where(lane_low, square[:virtual_rows], square[virtual_rows:])

    ready(1, 2, 3, 4, 5, 6)
    for p in range(pairs):
        c = p * 128
        k_pair, v_pair = k_ref[:, c:c + 128], v_ref[:, c:c + 128]
        vq = both_heads(virt_ref[:, c:c + 128])
        vcot = both_heads(vcot_ref[:, c:c + 128])
        scores = jnp.where(ok, nt(k_pair, vq * score_scale), NEG_FILL)
        attn = jnp.exp(scores - peak[p:p + 1]) * inv_total[p:p + 1]
        attn_hi = attn.astype(BF)
        attn_lo = (attn - attn_hi.astype(F32)).astype(BF)
        dw = nt(v_pair, vcot)
        ds = (attn * (dw - delta[p:p + 1]) * score_scale).astype(BF)
        vo_s[:, c:c + 128] = diagonal(tn(attn_hi, v_pair) + tn(attn_lo, v_pair))
        vgrad_s[0, :, c:c + 128] = diagonal(tn(ds, k_pair))
        dkw_s[n:2 * n, c:c + 128] = (dk_ref[0:n, c:c + 128] + nn(ds, vq)).astype(BF)
        dvw_s[n:2 * n, c:c + 128] = (dv_ref[0:n, c:c + 128] + nn(attn_hi, vcot)).astype(BF)
    out.send(dkw_s.at[own], kown_h)
    out.send(dvw_s.at[own], vown_h)
    vgrad_s[1] = dk_ref[n:n + virtual_rows, :]
    vgrad_s[2] = dv_ref[n:n + virtual_rows, :]
    ready(7, 8, 9, 10, 11, 12, 14, 15, 16, 17)
    vs = vs_ref[...]
    vg = None
    for t in range(3):
        part = vgrad_s[t]
        hi = part.astype(BF)
        lo = (part - hi.astype(F32)).astype(BF)
        if t == 0:
            wg = tn(xs_ref[n:2 * n, :], dq_ref[...])
        else:
            wg = tn(xs_ref[...], (dkw_s if t == 1 else dvw_s)[...])
        wg_s[t] = wg + (tn(vs, hi) + tn(vs, lo))
        back = nt(hi, w_ref[t]) + nt(lo, w_ref[t])
        vg = back if vg is None else vg + back
    vg_s[...] = vg
    row_groups = width // 64
    me = place()
    for half, ref, dst in ((1, send_s, send_h), (0, keep_s, keep_h)):
        for at in range(SHARDS // 2):
            shard = jnp.bitwise_xor(me, half * (SHARDS // 2) + at)
            cols = pl.ds(pl.multiple_of((shard // row_groups) * 128, 128), 128)
            group = lax.rem(shard, row_groups)
            for t in range(3):
                rows = pl.ds(pl.multiple_of(group * 64, 64), 64)
                ref[at, t * 64:(t + 1) * 64, :] = wg_s[t, rows, cols].astype(BF)
            rows = pl.ds(pl.multiple_of(group * 8, 8), 8)
            ref[at, 192:208, :] = jnp.concatenate([vg_s[rows, cols], vo_s[rows, cols]], axis=0).astype(BF)
        out.send(ref, dst)
    out.finish()


def node_kernel(w_h, dq_h, dk_h, dv_h, from_right_h, from_left_h, grad_h,
                w_ref, dq_ref, dk_ref, dv_ref, from_right, from_left, grad_s, sems):
    ready = loader((w_h, dq_h, dk_h, dv_h, from_right_h, from_left_h),
                   (w_ref, dq_ref, dk_ref, dv_ref, from_right, from_left), sems)
    out = Writer(sems, 6)
    ready(0, 1, 2, 3)
    part = nt(dq_ref[...], w_ref[0]) + nt(dk_ref[...], w_ref[1]) + nt(dv_ref[...], w_ref[2])
    ready(4, 5)
    grad_s[...] = (part + from_right[...].astype(F32) + from_left[...].astype(F32)).astype(BF)
    out.send(grad_s, grad_h)
    out.finish()


def unpack_kernel(p0_h, p1_h, wg_h, vg_h, vo_h, p0_ref, p1_ref, wg_s, vg_s, vo_s, vgb_s, vob_s, sems):
    width = wg_s.shape[2]
    row_groups = width // 64
    ready = loader((p0_h, p1_h), (p0_ref, p1_ref), sems)
    out = Writer(sems, 2)
    ready(0, 1)
    me = place()
    for t in range(3):
        for p in range(SHARDS):
            ref, at = (p0_ref, p1_ref)[p // (SHARDS // 2)], p % (SHARDS // 2)
            shard = jnp.bitwise_xor(me, p)
            cols = pl.ds(pl.multiple_of((shard // row_groups) * 128, 128), 128)
            group = lax.rem(shard, row_groups)
            rows = pl.ds(pl.multiple_of(group * 64, 64), 64)
            wg_s[t, rows, cols] = ref[at, t * 64:(t + 1) * 64, :].astype(F32)
            if t == 0:
                rows = pl.ds(pl.multiple_of(group * 8, 8), 8)
                both = ref[at, 192:208, :].astype(F32)
                vg_s[rows, cols] = both[0:8]
                vo_s[rows, cols] = both[8:16]
        out.send(wg_s.at[t], wg_h.at[t])
    vgb_s[...] = vg_s[...].astype(BF)
    vob_s[...] = vo_s[...].astype(BF)
    out.send(vgb_s, vg_h)
    out.send(vob_s, vo_h)
    out.finish()


ANY = pl.BlockSpec(memory_space=pl.ANY)


def call(body, args, outs, scratch, sems, flops=1e8, name=None, vmem=VMEM_BYTES):
    return pl.pallas_call(
        body,
        out_shape=[jax.ShapeDtypeStruct(s, d) for s, d in outs],
        in_specs=[ANY] * len(args),
        out_specs=[ANY] * len(outs),
        scratch_shapes=[pltpu.SMEM(s, d) if d == jnp.int32 else pltpu.VMEM(s, d) for s, d in scratch] + [pltpu.SemaphoreType.DMA((sems,))],
        compiler_params=pltpu.CompilerParams(vmem_limit_bytes=vmem),
        cost_estimate=pl.CostEstimate(flops=int(flops), bytes_accessed=4 << 20, transcendentals=0),
        name=name,
    )(*args)


def ring(value, steps):
    count = lax.axis_size("loop")
    return lax.ppermute(value, "loop", [(s, (s + steps) % count) for s in range(count)])


def swap(value, loop_bits, lane_bits):
    lanes = lax.axis_size("dp")
    count = lax.axis_size("loop") * lanes
    other = loop_bits * lanes + lane_bits
    return lax.ppermute(value, ("loop", "dp"), [(s, s ^ other) for s in range(count)])


def together(tree):
    return lax.optimization_barrier(tree)


PLANE = ((1, 2), (0, 2), (1, 0))
LINE = ((6, 0), (4, 0), (2, 0))


def total(parts):
    summed = parts[0].astype(F32)
    for part in parts[1:]:
        summed = summed + part.astype(F32)
    return summed.astype(BF)


def reduce_all(keep, send, node_step, middle):
    loop_size = lax.axis_size("loop")
    held = total([keep, swap(send, 0, 1)])
    held, middle = together((held, middle))
    quarters = [held[4 * j:4 * j + 4] for j in range(4)]
    got = [swap(quarters[3 - j], *bits) for j, bits in enumerate(PLANE)]
    got, middle = together((got, node_step(*middle)))
    held = together(total([quarters[0]] + got))
    got = together([swap(held[3 - j], *bits) for j, bits in enumerate(LINE)])
    piece = total([held[0]] + got)
    bit = 8
    while bit < loop_size:
        piece = total([piece, swap(piece, bit, 0)])
        bit *= 2
    piece = together(piece)
    got = together([swap(piece, *bits) for bits in LINE])
    held = together(jnp.stack([piece] + got[::-1]))
    got = together([swap(held, *bits) for bits in PLANE])
    held = together(jnp.concatenate([held] + got[::-1], axis=0))
    return held, swap(held, 0, 1), middle


def local(node_states, virtual_states, projection, pattern, valid_counts, node_cotangent, virtual_cotangent):
    n, width = node_states.shape
    blocks = pattern.shape[0]
    block_rows = n // blocks
    virtual_rows = virtual_states.shape[0]
    loop_size, lanes = lax.axis_size("loop"), lax.axis_size("dp")
    devices = loop_size * lanes
    score_scale = (width // H) ** -0.5
    keys = 3 * n + virtual_rows

    shape = (blocks, block_rows, width)
    valid = lax.broadcasted_iota(jnp.int32, shape, 1) < lax.broadcast_in_dim(valid_counts, shape, (0,))
    marked = jnp.where(valid, node_states.reshape(shape), jnp.asarray(ABSENT, BF)).reshape(n, width)
    x_left, x_right = ring(marked, 1), ring(marked, -1)

    counts_i, pattern_i = ((blocks,), jnp.int32), (pattern.shape, jnp.int32)
    rows_bf, rows_f = ((n, width), BF), ((n, width), F32)
    wide = ((3, width, width), BF)
    virt_bf, virt_f = ((virtual_rows, width), BF), ((virtual_rows, width), F32)
    triple = ((3, virtual_rows, width), BF)
    stats_f = ((devices, 16, 128), F32)
    q, k, v, virt, stats = call(
        functools.partial(project_kernel, blocks, block_rows, score_scale),
        (valid_counts, node_states, projection, virtual_states, virtual_cotangent),
        [rows_bf] * 3 + [triple, stats_f],
        [rows_bf, wide, virt_bf, virt_bf] + [rows_bf] * 3 + [triple, stats_f, counts_i], 12, name="project")
    stats = lax.all_to_all(stats, ("loop", "dp"), 0, 0, tiled=True)

    keys_bf = ((keys, width), BF)
    across = ((width, n), F32)
    near_bf, mine_f = ((2 * n, width), BF), ((n + virtual_rows, width), F32)
    node_out, dq, to_left, to_right, dkn, dvn, dko, dvo = call(
        functools.partial(attention_kernel, blocks, block_rows, score_scale),
        (pattern, valid_counts, x_left, x_right, projection, q, k, v, node_cotangent, virt),
        [rows_bf] * 4 + [near_bf] * 2 + [mine_f] * 2,
        [rows_bf] * 2 + [((2, width, width), BF)] + [rows_bf] * 2
        + [keys_bf] * 2 + [((keys, n), F32), across, across] + [rows_bf] * 2 + [near_bf] * 2 + [mine_f] * 2 + [rows_bf] * 2
        + [pattern_i, counts_i], 20,
        flops=4e9, name="attention")
    from_right, from_left = ring(to_left, -1), ring(to_right, 1)

    window_bf = ((3 * n, width), BF)
    half = ((SHARDS // 2, 3 * 64 + 16, 128), BF)
    keep, send, dk, dv = call(
        functools.partial(weight_kernel, blocks, block_rows, score_scale),
        (valid_counts, node_states, x_left, x_right, virtual_states, virtual_cotangent, projection, k, v, virt, stats,
         dq, dkn, dvn, dko, dvo),
        [half] * 2 + [rows_bf] * 2,
        [window_bf, virt_bf, virt_bf, wide, rows_bf, rows_bf, virt_bf, stats_f, rows_bf, mine_f, mine_f]
        + [half] * 2 + [((3, width, width), F32), virt_f, virt_f, ((3, virtual_rows, width), F32), window_bf, window_bf, counts_i], 24,
        flops=8e9, name="weight_grads")
    def node_step(*args):
        return call(node_kernel, args, [rows_bf], [wide] + [rows_bf] * 6, 7, flops=1e9, name="node_grads")[0]

    send, from_right, from_left = together((send, from_right, from_left))
    mine, other, node_grad = reduce_all(keep, send, node_step, (projection, dq, dk, dv, from_right, from_left))
    weight_grads, virtual_grad, virtual_out = call(
        unpack_kernel, (mine, other), [((3, width, width), F32), virt_bf, virt_bf],
        [half, half, ((3, width, width), F32), virt_f, virt_f, virt_bf, virt_bf], 7, name="unpack",
        vmem=16 << 20)
    return node_out, virtual_out, node_grad, virtual_grad, weight_grads


def solution(mesh):
    return jax.shard_map(
        local,
        mesh=mesh,
        in_specs=(
            P(("loop", "dp"), None),
            P(),
            P(),
            P(("loop", "dp"), None),
            P(("loop", "dp")),
            P(("loop", "dp"), None),
            P(),
        ),
        out_specs=(P(("loop", "dp"), None), P(), P(("loop", "dp"), None), P(), P()),
        check_vma=False,
    )
```

```python
import functools

import jax
import jax.numpy as jnp
from jax import lax
from jax.experimental import pallas as pl
from jax.experimental.pallas import tpu as pltpu
from jax.sharding import PartitionSpec as P

H = 8
NEG_FILL = -1e30
SHARDS = 32
ABSENT = 1000.0
VMEM_BYTES = 60 << 20
BF = jnp.bfloat16
F32 = jnp.float32


def nn(a, b):
    return lax.dot_general(a, b, (((1,), (0,)), ((), ())), preferred_element_type=F32)


def nt(a, b):
    return lax.dot_general(a, b, (((1,), (1,)), ((), ())), preferred_element_type=F32)


def tn(a, b):
    return lax.dot_general(a, b, (((0,), (0,)), ((), ())), preferred_element_type=F32)


def lane_half(pair, half):
    lane = lax.broadcasted_iota(jnp.int32, pair.shape, 1)
    width = pair.shape[1] // 2
    keep = lane < width if half == 0 else lane >= width
    return jnp.where(keep, pair, jnp.zeros_like(pair))


def both_heads(pair):
    return jnp.concatenate([lane_half(pair, 0), lane_half(pair, 1)], axis=0)


def own_row_ok(counts_ref, blocks, block_rows, shape):
    row = lax.broadcasted_iota(jnp.int32, shape, 0)
    limit = jnp.full(shape, counts_ref[0], jnp.int32)
    for b in range(1, blocks):
        limit = jnp.where(row < b * block_rows, limit, b * block_rows + counts_ref[b])
    return row < limit


def loader(srcs, dsts, sems):
    copies = [pltpu.make_async_copy(src, dst, sems.at[i]) for i, (src, dst) in enumerate(zip(srcs, dsts))]
    for copy in copies:
        copy.start()

    def ready(*which):
        for i in which:
            copies[i].wait()

    return ready


class Writer:
    def __init__(self, sems, base):
        self.sems, self.base, self.copies = sems, base, []

    def send(self, src, dst):
        copy = pltpu.make_async_copy(src, dst, self.sems.at[self.base + len(self.copies)])
        copy.start()
        self.copies.append(copy)

    def finish(self):
        for copy in self.copies:
            copy.wait()


def place():
    loop_here, lane_here = lax.axis_index("loop"), lax.axis_index("dp")
    core, x_at = lane_here & 1, (lane_here >> 1) & 1
    y_at, z_at = loop_here & 1, (loop_here >> 1) & 3
    return core * 16 + x_at * 8 + y_at * 4 + z_at


def project_kernel(blocks, block_rows, score_scale, counts_h, x_h, w_h, vs_h, vcot_h,
                   q_h, k_h, v_h, virt_h, stats_h, x_ref, w_ref, vs_ref, vcot_ref, q_s, k_s, v_s, virt_s, stats_s, counts_ref, sems):
    ready = loader((x_h, w_h.at[1], w_h.at[2], vs_h, w_h.at[0], vcot_h, counts_h),
                   (x_ref, w_ref.at[1], w_ref.at[2], vs_ref, w_ref.at[0], vcot_ref, counts_ref), sems)
    out = Writer(sems, 7)
    ready(0, 1, 2)
    x = x_ref[...]
    k = nn(x, w_ref[1]).astype(BF)
    v = nn(x, w_ref[2]).astype(BF)
    k_s[...] = k
    v_s[...] = v
    out.send(k_s, k_h)
    out.send(v_s, v_h)
    ready(3, 4, 5, 6)
    virt_q = nn(vs_ref[...], w_ref[0]).astype(BF)
    virt_s[0] = virt_q
    virt_s[1] = nn(vs_ref[...], w_ref[1]).astype(BF)
    virt_s[2] = nn(vs_ref[...], w_ref[2]).astype(BF)
    out.send(virt_s, virt_h)
    virt_q = virt_q * score_scale
    n, width = x.shape
    ok = own_row_ok(counts_ref, blocks, block_rows, (n, 128))
    peaks, totals, deltas = [], [], []
    for c in range(0, width, 128):
        scores = nt(k[:, c:c + 128], both_heads(virt_q[:, c:c + 128]))
        scores = jnp.where(ok, scores, NEG_FILL)
        peak = jnp.max(scores, axis=0, keepdims=True)
        e = jnp.where(ok, jnp.exp(scores - peak), 0.0)
        dw = nt(v[:, c:c + 128], both_heads(vcot_ref[:, c:c + 128]))
        peaks.append(peak)
        totals.append(jnp.sum(e, axis=0, keepdims=True))
        deltas.append(jnp.sum(e * dw, axis=0, keepdims=True))
    rows = jnp.concatenate(peaks + totals + deltas + peaks, axis=0)
    stats_s[...] = jnp.broadcast_to(rows[None], stats_s.shape)
    out.send(stats_s, stats_h)
    q_s[...] = nn(x, w_ref[0]).astype(BF) * score_scale
    out.send(q_s, q_h)
    out.finish()


def attention_kernel(blocks, block_rows, score_scale, pat_h, co_h, xl_h, xr_h,
                     w_h, q_h, k_h, v_h, g_h, virt_h,
                     out_h, dq_h, left_h, right_h, dkn_h, dvn_h, dko_h, dvo_h,
                     xl_ref, xr_ref, w_ref, q_ref, g_ref,
                     key_s, val_s, bias_s, ot_s, dqt_s, out_s, dq_s, dkn_s, dvn_s, dko_s, dvo_s, left_s, right_s, s_s, dw_s, wt_s, ds_s, pat_ref, co_ref, sems):
    n, width = q_ref.shape
    virtual_rows, keys = virt_h.shape[1], key_s.shape[0]
    loop_here, loop_size, lanes = lax.axis_index("loop"), lax.axis_size("loop"), lax.axis_size("dp")
    own, virt = pl.ds(n, n), pl.ds(3 * n, virtual_rows)
    ready = loader((xl_h, xr_h, w_h.at[1], w_h.at[2], k_h, v_h, virt_h.at[1], virt_h.at[2], q_h, g_h, pat_h, co_h),
                   (xl_ref, xr_ref, w_ref.at[0], w_ref.at[1], key_s.at[own], val_s.at[own],
                    key_s.at[virt], val_s.at[virt], q_ref, g_ref, pat_ref, co_ref), sems)
    out = Writer(sems, 12)
    row = lax.broadcasted_iota(jnp.int32, (block_rows, block_rows), 0)
    bias_s[3 * n:3 * n + virtual_rows, :] = jnp.zeros((virtual_rows, n), F32)
    ready(0, 1, 10, 11)
    for i in range(blocks):
        slots = []
        for j in range(pat_ref.shape[1]):
            block = pat_ref[i, j]
            ring_at = (block // blocks) // lanes
            offset = lax.rem(ring_at - loop_here + 1 + 2 * loop_size, loop_size)
            slots.append(offset * blocks + lax.rem(block, blocks))
        for b in range(3 * blocks):
            listed = slots[0] == b
            for s in slots[1:]:
                listed = jnp.logical_or(listed, s == b)
            at, inner = b // blocks, b % blocks
            if at == 1:
                okb = row < jnp.where(listed, co_ref[inner], 0)
            else:
                x_ref = (xl_ref, None, xr_ref)[at]
                mark = x_ref[inner * block_rows:(inner + 1) * block_rows, 0:128].astype(F32)[:, 0:1]
                okb = jnp.broadcast_to(mark, (block_rows, block_rows)) < jnp.where(listed, 0.5 * ABSENT, -ABSENT)
            bias_s[b * block_rows:(b + 1) * block_rows, i * block_rows:(i + 1) * block_rows] = jnp.where(
                okb, 0.0, NEG_FILL)
    ready(2, 3)
    for at, ref in ((0, xl_ref), (2, xr_ref)):
        x = ref[...]
        key_s[at * n:(at + 1) * n, :] = nn(x, w_ref[0]).astype(BF)
        val_s[at * n:(at + 1) * n, :] = nn(x, w_ref[1]).astype(BF)
    ready(4, 5, 6, 7, 8, 9)
    ok = own_row_ok(co_ref, blocks, block_rows, (n, 128))
    for c in range(0, width, 128):
        k_pair, v_pair = key_s[:, c:c + 128], val_s[:, c:c + 128]
        q_pair = q_ref[:, c:c + 128]
        g_pair = jnp.where(ok, g_ref[:, c:c + 128], jnp.zeros((n, 128), BF))
        k_t, v_t = k_pair.T, v_pair.T
        masked = [(lane_half(q_pair, half), lane_half(g_pair, half)) for half in range(2)]
        for half, (qm, gm) in enumerate(masked):
            s_s[half] = nt(k_pair, qm) + bias_s[...]
            dw_s[half] = nt(v_pair, gm)
        dk_pair = dv_pair = None
        for half, (qm, gm) in enumerate(masked):
            peak = jnp.full((8, n), NEG_FILL, F32)
            for r in range(0, keys, 64):
                peak = jnp.maximum(peak, jnp.max(s_s[half, r:r + 64, :].reshape(64 // 8, 8, n), axis=0))
            peak = jnp.max(peak, axis=0, keepdims=True)
            total8 = delta8 = jnp.zeros((8, n), F32)
            for r in range(0, keys, 64):
                e = jnp.exp(s_s[half, r:r + 64, :] - peak)
                s_s[half, r:r + 64, :] = e
                total8 = total8 + jnp.sum(e.reshape(64 // 8, 8, n), axis=0)
                delta8 = delta8 + jnp.sum((e * dw_s[half, r:r + 64, :]).reshape(64 // 8, 8, n), axis=0)
            inv = 1.0 / jnp.sum(total8, axis=0, keepdims=True)
            delta = jnp.sum(delta8, axis=0, keepdims=True) * inv
            for r in range(0, keys, 64):
                a = s_s[half, r:r + 64, :] * inv
                wt_s[half, r:r + 64, :] = a.astype(BF)
                ds_s[half, r:r + 64, :] = (a * (dw_s[half, r:r + 64, :] - delta)).astype(BF)
            wt, ds = wt_s[half], ds_s[half]
            at = c + half * 64
            ot_s[at:at + 64, :] = nn(v_t[half * 64:half * 64 + 64], wt)
            dqt_s[at:at + 64, :] = nn(k_t[half * 64:half * 64 + 64], ds)
            dk, dv = nn(ds, qm), nn(wt, gm)
            dk_pair = dk if dk_pair is None else dk_pair + dk
            dv_pair = dv if dv_pair is None else dv_pair + dv
        for near, mine, part in ((dkn_s, dko_s, dk_pair), (dvn_s, dvo_s, dv_pair)):
            near[0:n, c:c + 128] = part[0:n].astype(BF)
            near[n:2 * n, c:c + 128] = part[2 * n:3 * n].astype(BF)
            mine[0:n, c:c + 128] = part[n:2 * n]
            mine[n:n + virtual_rows, c:c + 128] = part[3 * n:3 * n + virtual_rows]
        dq_s[:, c:c + 128] = (dqt_s[c:c + 128, :] * score_scale).astype(BF).T
        out_s[:, c:c + 128] = jnp.where(ok, ot_s[c:c + 128, :].astype(BF).T, jnp.zeros((n, 128), BF))
        cols = pl.ds(c, 128)
        for src, dst in ((dkn_s, dkn_h), (dvn_s, dvn_h), (dko_s, dko_h), (dvo_s, dvo_h), (dq_s, dq_h), (out_s, out_h)):
            out.send(src.at[:, cols], dst.at[:, cols])
    for rows, ref, dst in ((slice(0, n), left_s, left_h), (slice(n, 2 * n), right_s, right_h)):
        ref[...] = (nt(dkn_s[rows, :], w_ref[0]) + nt(dvn_s[rows, :], w_ref[1])).astype(BF)
        out.send(ref, dst)
    out.finish()


def weight_kernel(blocks, block_rows, score_scale, counts_h, x_h, xl_h, xr_h, vs_h, vcot_h, w_h,
                  k_h, v_h, virt_h, stats_h, dq_h, dkn_h, dvn_h, dko_h, dvo_h,
                  keep_h, send_h, kown_h, vown_h,
                  xs_ref, vcot_ref, w_ref, k_ref, v_ref, virt_ref, stats_ref, dko_ref, dvo_ref,
                  xt_s, dqw_s, dkw_s, dvw_s, pack_s, counts_ref, sems):
    n, width = x_h.shape
    virtual_rows = vs_h.shape[0]
    near, own, last = pl.ds(0, 2 * n), pl.ds(2 * n, n), pl.ds(3 * n, virtual_rows)
    ready = loader((xl_h, xr_h, x_h, vs_h, stats_h, counts_h, k_h, v_h, virt_h.at[0], vcot_h, dko_h, dvo_h,
                    dq_h, dkn_h, dvn_h, w_h),
                   (xs_ref.at[pl.ds(0, n)], xs_ref.at[pl.ds(n, n)], xs_ref.at[own], xs_ref.at[last], stats_ref, counts_ref,
                    k_ref, v_ref, virt_ref, vcot_ref, dko_ref, dvo_ref,
                    dqw_s.at[pl.ds(0, n)], dkw_s.at[near], dvw_s.at[near], w_ref), sems)
    out = Writer(sems, 16)
    pairs = width // 128
    ready(0, 1, 2, 3)
    for c in range(0, width, 128):
        xt_s[c:c + 128, :] = xs_ref[:, c:c + 128].T
    ready(4, 5)
    ok = own_row_ok(counts_ref, blocks, block_rows, (n, 128))
    stats = stats_ref[...]
    peak = jnp.max(stats[:, 0:pairs], axis=0)
    factor = jnp.exp(stats[:, 0:pairs] - peak[None])
    total = jnp.sum(stats[:, pairs:2 * pairs] * factor, axis=0)
    delta = jnp.sum(stats[:, 2 * pairs:3 * pairs] * factor, axis=0) / total
    inv_total = 1.0 / total
    lane_low = lax.broadcasted_iota(jnp.int32, (virtual_rows, 128), 1) < 64

    def diagonal(square):
        return jnp.where(lane_low, square[:virtual_rows], square[virtual_rows:])

    ready(6, 7, 8, 9, 10, 11)
    mixed = []
    for p in range(pairs):
        c = p * 128
        k_pair, v_pair = k_ref[:, c:c + 128], v_ref[:, c:c + 128]
        vq = both_heads(virt_ref[:, c:c + 128])
        vcot = both_heads(vcot_ref[:, c:c + 128])
        scores = jnp.where(ok, nt(k_pair, vq * score_scale), NEG_FILL)
        attn = jnp.exp(scores - peak[p:p + 1]) * inv_total[p:p + 1]
        attn_bf = attn.astype(BF)
        dw = nt(v_pair, vcot)
        ds = (attn * (dw - delta[p:p + 1]) * score_scale).astype(BF)
        mixed.append(diagonal(tn(attn_bf, v_pair)))
        dqw_s[n:n + virtual_rows, c:c + 128] = diagonal(tn(ds, k_pair)).astype(BF)
        dkw_s[2 * n:3 * n, c:c + 128] = (dko_ref[0:n, c:c + 128] + nn(ds, vq)).astype(BF)
        dvw_s[2 * n:3 * n, c:c + 128] = (dvo_ref[0:n, c:c + 128] + nn(attn_bf, vcot)).astype(BF)
    dkw_s[3 * n:3 * n + virtual_rows, :] = dko_ref[n:n + virtual_rows, :].astype(BF)
    dvw_s[3 * n:3 * n + virtual_rows, :] = dvo_ref[n:n + virtual_rows, :].astype(BF)
    out.send(dkw_s.at[own], kown_h)
    out.send(dvw_s.at[own], vown_h)
    ready(12, 13, 14)
    me = place()
    row_groups = width // 64
    for c in range(0, width, 256):
        for t in range(3):
            if t == 0:
                wg = nn(xt_s[:, 2 * n:], dqw_s[:, c:c + 256])
            else:
                wg = nn(xt_s[...], (dkw_s if t == 1 else dvw_s)[:, c:c + 256])
            for col in range(0, 256, 128):
                for group in range(row_groups):
                    at = jnp.bitwise_xor(me, (c + col) // 128 * row_groups + group)
                    pack_s[at, t * 64:(t + 1) * 64, :] = wg[group * 64:(group + 1) * 64, col:col + 128].astype(BF)
    ready(15)
    vg = (nt(dqw_s[n:n + virtual_rows, :], w_ref[0]) + nt(dkw_s[3 * n:3 * n + virtual_rows, :], w_ref[1])
          + nt(dvw_s[3 * n:3 * n + virtual_rows, :], w_ref[2]))
    for p in range(pairs):
        for group in range(row_groups):
            at = jnp.bitwise_xor(me, p * row_groups + group)
            rows = slice(group * 8, group * 8 + 8)
            pack_s[at, 192:208, :] = jnp.concatenate(
                [vg[rows, p * 128:(p + 1) * 128], mixed[p][rows]], axis=0).astype(BF)
    out.send(pack_s.at[pl.ds(SHARDS // 2, SHARDS // 2)], send_h)
    out.send(pack_s.at[pl.ds(0, SHARDS // 2)], keep_h)
    out.finish()


def node_kernel(w_h, dq_h, dk_h, dv_h, part_h, w_ref, dq_ref, dk_ref, dv_ref, part_s, sems):
    ready = loader((w_h, dq_h, dk_h, dv_h), (w_ref, dq_ref, dk_ref, dv_ref), sems)
    out = Writer(sems, 4)
    ready(0, 1, 2, 3)
    part_s[...] = nt(dq_ref[...], w_ref[0]) + nt(dk_ref[...], w_ref[1]) + nt(dv_ref[...], w_ref[2])
    out.send(part_s, part_h)
    out.finish()


def unpack_kernel(second, part_h, *refs):
    wg_h, vg_h, vo_h, part_ref, wg_s, vg_s, vo_s, vgb_s, vob_s, sems = refs[3 * second:]
    row_groups = wg_s.shape[1] // 64
    ready = loader((part_h,), (part_ref,), sems)
    out = Writer(sems, 1)
    me = jnp.bitwise_and(place(), SHARDS // 2 - 1)
    core = jnp.bitwise_and(lax.axis_index("dp"), 1)
    if second:
        core = 1 - core
    half = wg_s.shape[2]
    columns = pl.ds(pl.multiple_of(core * half, half), half)
    ready(0)
    for t in range(3):
        for p in range(SHARDS // 2):
            shard = jnp.bitwise_xor(me, p)
            cols = pl.ds(pl.multiple_of((shard // row_groups) * 128, 128), 128)
            group = lax.rem(shard, row_groups)
            rows = pl.ds(pl.multiple_of(group * 64, 64), 64)
            wg_s[t, rows, cols] = part_ref[p, t * 64:(t + 1) * 64, :].astype(F32)
            if t == 0:
                rows = pl.ds(pl.multiple_of(group * 8, 8), 8)
                both = part_ref[p, 192:208, :].astype(F32)
                vg_s[rows, cols] = both[0:8]
                vo_s[rows, cols] = both[8:16]
        out.send(wg_s.at[t], wg_h.at[t, :, columns])
    vgb_s[...] = vg_s[...].astype(BF)
    vob_s[...] = vo_s[...].astype(BF)
    out.send(vgb_s, vg_h.at[:, columns])
    out.send(vob_s, vo_h.at[:, columns])
    out.finish()


ANY = pl.BlockSpec(memory_space=pl.ANY)


def call(body, args, outs, scratch, sems, flops=1e8, name=None, vmem=VMEM_BYTES, aliases=None):
    return pl.pallas_call(
        body,
        out_shape=[jax.ShapeDtypeStruct(s, d) for s, d in outs],
        in_specs=[ANY] * len(args),
        out_specs=[ANY] * len(outs),
        scratch_shapes=[pltpu.SMEM(s, d) if d == jnp.int32 else pltpu.VMEM(s, d) for s, d in scratch] + [pltpu.SemaphoreType.DMA((sems,))],
        compiler_params=pltpu.CompilerParams(vmem_limit_bytes=vmem),
        cost_estimate=pl.CostEstimate(flops=int(flops), bytes_accessed=4 << 20, transcendentals=0),
        input_output_aliases=aliases or {},
        name=name,
    )(*args)


def ring(value, steps):
    count = lax.axis_size("loop")
    return lax.ppermute(value, "loop", [(s, (s + steps) % count) for s in range(count)])


def swap(value, loop_bits, lane_bits):
    lanes = lax.axis_size("dp")
    count = lax.axis_size("loop") * lanes
    other = loop_bits * lanes + lane_bits
    return lax.ppermute(value, ("loop", "dp"), [(s, s ^ other) for s in range(count)])


def together(tree):
    return lax.optimization_barrier(tree)


PLANE = ((1, 2), (0, 2), (1, 0))
LINE = ((6, 0), (4, 0), (2, 0))


def total(parts):
    summed = parts[0].astype(F32)
    for part in parts[1:]:
        summed = summed + part.astype(F32)
    return summed.astype(BF)


def reduce_all(keep, send, own_part, to_left, to_right):
    loop_size = lax.axis_size("loop")
    held = total([keep, swap(send, 0, 1)])
    held = together(held)
    quarters = [held[4 * j:4 * j + 4] for j in range(4)]
    got = [swap(quarters[3 - j], *bits) for j, bits in enumerate(PLANE)]
    got, own_part = together((got, own_part))
    held, to_left, to_right = together((total([quarters[0]] + got), to_left, to_right))
    from_right, from_left = ring(to_left, -1), ring(to_right, 1)
    got = together([swap(held[3 - j], *bits) for j, bits in enumerate(LINE)])
    piece = total([held[0]] + got)
    bit = 8
    while bit < loop_size:
        piece = total([piece, swap(piece, bit, 0)])
        bit *= 2
    piece = together(piece)
    got, from_right, from_left = together(([swap(piece, *bits) for bits in LINE], from_right, from_left))
    held = together(jnp.stack([piece] + got[::-1]))
    got, node_grad = together(([swap(held, *bits) for bits in PLANE], total([own_part, from_right, from_left])))
    held = together(jnp.concatenate([held] + got[::-1], axis=0))
    return held, swap(held, 0, 1), node_grad


def local(node_states, virtual_states, projection, pattern, valid_counts, node_cotangent, virtual_cotangent):
    n, width = node_states.shape
    blocks = pattern.shape[0]
    block_rows = n // blocks
    virtual_rows = virtual_states.shape[0]
    loop_size, lanes = lax.axis_size("loop"), lax.axis_size("dp")
    devices = loop_size * lanes
    score_scale = (width // H) ** -0.5
    keys = 3 * n + virtual_rows

    shape = (blocks, block_rows, width)
    place_in_block = lax.broadcasted_iota(jnp.int32, shape, 1) * width + lax.broadcasted_iota(jnp.int32, shape, 2)
    valid = place_in_block < lax.broadcast_in_dim(valid_counts * width, shape, (0,))
    marked = jnp.where(valid, node_states.reshape(shape), jnp.asarray(ABSENT, BF)).reshape(n, width)
    x_left, x_right = ring(marked, 1), ring(marked, -1)

    counts_i, pattern_i = ((blocks,), jnp.int32), (pattern.shape, jnp.int32)
    rows_bf, rows_f = ((n, width), BF), ((n, width), F32)
    wide = ((3, width, width), BF)
    virt_bf, virt_f = ((virtual_rows, width), BF), ((virtual_rows, width), F32)
    triple = ((3, virtual_rows, width), BF)
    stats_f = ((devices, 16, 128), F32)
    q, k, v, virt, stats = call(
        functools.partial(project_kernel, blocks, block_rows, score_scale),
        (valid_counts, node_states, projection, virtual_states, virtual_cotangent),
        [rows_bf] * 3 + [triple, stats_f],
        [rows_bf, wide, virt_bf, virt_bf] + [rows_bf] * 3 + [triple, stats_f, counts_i], 12, name="project")
    stats = lax.all_to_all(stats, ("loop", "dp"), 0, 0, tiled=True)

    keys_bf = ((keys, width), BF)
    across = ((width, n), F32)
    near_bf, mine_f = ((2 * n, width), BF), ((n + virtual_rows, width), F32)
    node_out, dq, to_left, to_right, dkn, dvn, dko, dvo = call(
        functools.partial(attention_kernel, blocks, block_rows, score_scale),
        (pattern, valid_counts, x_left, x_right, projection, q, k, v, node_cotangent, virt),
        [rows_bf] * 4 + [near_bf] * 2 + [mine_f] * 2,
        [rows_bf] * 2 + [((2, width, width), BF)] + [rows_bf] * 2
        + [keys_bf] * 2 + [((keys, n), F32), across, across] + [rows_bf] * 2 + [near_bf] * 2 + [mine_f] * 2 + [rows_bf] * 2
        + [((2, keys, n), F32)] * 2 + [((2, keys, n), BF)] * 2 + [pattern_i, counts_i], 40,
        flops=4e9, name="attention")
    to_left, to_right, stats = together((to_left, to_right, stats))

    half = ((SHARDS // 2, 3 * 64 + 16, 128), BF)
    keep, send, dk, dv = call(
        functools.partial(weight_kernel, blocks, block_rows, score_scale),
        (valid_counts, node_states, x_left, x_right, virtual_states, virtual_cotangent, projection, k, v, virt, stats,
         dq, dkn, dvn, dko, dvo),
        [half] * 2 + [rows_bf] * 2,
        [keys_bf, virt_bf, wide, rows_bf, rows_bf, virt_bf, stats_f, mine_f, mine_f,
         ((width, keys), BF), ((n + virtual_rows, width), BF), keys_bf, keys_bf, ((SHARDS, 3 * 64 + 16, 128), BF), counts_i], 20,
        flops=8e9, name="weight_grads")
    own_part, = call(node_kernel, (projection, dq, dk, dv), [rows_f], [wide] + [rows_bf] * 3 + [rows_f], 5,
                     flops=1e9, name="node_grads")
    mine, other, node_grad = reduce_all(keep, send, own_part, to_left, to_right)
    halves_f = ((virtual_rows, width // 2), F32)
    unpack = functools.partial(
        call, outs=[((3, width, width), F32), virt_bf, virt_bf],
        scratch=[half, ((3, width, width // 2), F32), halves_f, halves_f] + [((virtual_rows, width // 2), BF)] * 2, sems=6,
        vmem=16 << 20)
    results = unpack(functools.partial(unpack_kernel, 0), (mine,), name="unpack_mine")
    weight_grads, virtual_grad, virtual_out = unpack(
        functools.partial(unpack_kernel, 1), (other, *results), name="unpack_other", aliases={1: 0, 2: 1, 3: 2})
    return node_out, virtual_out, node_grad, virtual_grad, weight_grads


def solution(mesh):
    return jax.shard_map(
        local,
        mesh=mesh,
        in_specs=(
            P(("loop", "dp"), None),
            P(),
            P(),
            P(("loop", "dp"), None),
            P(("loop", "dp")),
            P(("loop", "dp"), None),
            P(),
        ),
        out_specs=(P(("loop", "dp"), None), P(), P(("loop", "dp"), None), P(), P()),
        check_vma=False,
    )
```

```python
import functools

import jax
import jax.numpy as jnp
from jax import lax
from jax.experimental import pallas as pl
from jax.experimental.pallas import tpu as pltpu
from jax.sharding import PartitionSpec as P

H = 8
NEG_FILL = -1e30
SHARDS = 32
ABSENT = 1000.0
VMEM_BYTES = 60 << 20
BF = jnp.bfloat16
F32 = jnp.float32


def nn(a, b):
    return lax.dot_general(a, b, (((1,), (0,)), ((), ())), preferred_element_type=F32)


def nt(a, b):
    return lax.dot_general(a, b, (((1,), (1,)), ((), ())), preferred_element_type=F32)


def tn(a, b):
    return lax.dot_general(a, b, (((0,), (0,)), ((), ())), preferred_element_type=F32)


def lane_half(pair, half):
    lane = lax.broadcasted_iota(jnp.int32, pair.shape, 1)
    width = pair.shape[1] // 2
    keep = lane < width if half == 0 else lane >= width
    return jnp.where(keep, pair, jnp.zeros_like(pair))


def both_heads(pair):
    return jnp.concatenate([lane_half(pair, 0), lane_half(pair, 1)], axis=0)


def own_row_ok(counts_ref, blocks, block_rows, shape):
    row = lax.broadcasted_iota(jnp.int32, shape, 0)
    limit = jnp.full(shape, counts_ref[0], jnp.int32)
    for b in range(1, blocks):
        limit = jnp.where(row < b * block_rows, limit, b * block_rows + counts_ref[b])
    return row < limit


def loader(srcs, dsts, sems):
    copies = [pltpu.make_async_copy(src, dst, sems.at[i]) for i, (src, dst) in enumerate(zip(srcs, dsts))]
    for copy in copies:
        copy.start()

    def ready(*which):
        for i in which:
            copies[i].wait()

    return ready


class Writer:
    def __init__(self, sems, base):
        self.sems, self.base, self.copies = sems, base, []

    def send(self, src, dst):
        copy = pltpu.make_async_copy(src, dst, self.sems.at[self.base + len(self.copies)])
        copy.start()
        self.copies.append(copy)

    def finish(self):
        for copy in self.copies:
            copy.wait()


def place():
    loop_here, lane_here = lax.axis_index("loop"), lax.axis_index("dp")
    core, x_at = lane_here & 1, (lane_here >> 1) & 1
    y_at, z_at = loop_here & 1, (loop_here >> 1) & 3
    return core * 16 + x_at * 8 + y_at * 4 + z_at


def project_kernel(blocks, block_rows, score_scale, counts_h, x_h, w_h, vs_h, vcot_h,
                   q_h, k_h, v_h, virt_h, stats_h, x_ref, w_ref, vs_ref, vcot_ref, q_s, k_s, v_s, virt_s, stats_s, counts_ref, sems):
    ready = loader((x_h, w_h.at[1], w_h.at[2], vs_h, w_h.at[0], vcot_h, counts_h),
                   (x_ref, w_ref.at[1], w_ref.at[2], vs_ref, w_ref.at[0], vcot_ref, counts_ref), sems)
    out = Writer(sems, 7)
    ready(0, 1, 2)
    x = x_ref[...]
    k = nn(x, w_ref[1]).astype(BF)
    v = nn(x, w_ref[2]).astype(BF)
    k_s[...] = k
    v_s[...] = v
    out.send(k_s, k_h)
    out.send(v_s, v_h)
    ready(3, 4, 5, 6)
    virt_q = nn(vs_ref[...], w_ref[0]).astype(BF)
    virt_s[0] = virt_q
    virt_s[1] = nn(vs_ref[...], w_ref[1]).astype(BF)
    virt_s[2] = nn(vs_ref[...], w_ref[2]).astype(BF)
    out.send(virt_s, virt_h)
    virt_q = virt_q * score_scale
    n, width = x.shape
    ok = own_row_ok(counts_ref, blocks, block_rows, (n, 128))
    peaks, totals, deltas = [], [], []
    for c in range(0, width, 128):
        scores = nt(k[:, c:c + 128], both_heads(virt_q[:, c:c + 128]))
        scores = jnp.where(ok, scores, NEG_FILL)
        peak = jnp.max(scores, axis=0, keepdims=True)
        e = jnp.where(ok, jnp.exp(scores - peak), 0.0)
        dw = nt(v[:, c:c + 128], both_heads(vcot_ref[:, c:c + 128]))
        peaks.append(peak)
        totals.append(jnp.sum(e, axis=0, keepdims=True))
        deltas.append(jnp.sum(e * dw, axis=0, keepdims=True))
    rows = jnp.concatenate(peaks + totals + deltas + peaks, axis=0)
    stats_s[...] = jnp.broadcast_to(rows[None], stats_s.shape)
    out.send(stats_s, stats_h)
    q_s[...] = nn(x, w_ref[0]).astype(BF) * score_scale
    out.send(q_s, q_h)
    out.finish()


def fill_bias(blocks, block_rows, pat_ref, co_ref, xs_ref, bias_s):
    n = blocks * block_rows
    loop_here, loop_size, lanes = lax.axis_index("loop"), lax.axis_size("loop"), lax.axis_size("dp")
    row = lax.broadcasted_iota(jnp.int32, (block_rows, block_rows), 0)
    bias_s[3 * n:, :] = jnp.zeros((bias_s.shape[0] - 3 * n, n), F32)
    for i in range(blocks):
        slots = []
        for j in range(pat_ref.shape[1]):
            block = pat_ref[i, j]
            ring_at = (block // blocks) // lanes
            offset = lax.rem(ring_at - loop_here + 1 + 2 * loop_size, loop_size)
            slots.append(offset * blocks + lax.rem(block, blocks))
        for b in range(3 * blocks):
            listed = slots[0] == b
            for s in slots[1:]:
                listed = jnp.logical_or(listed, s == b)
            inner = b % blocks
            first = (0, 2 * n, n)[b // blocks] + inner * block_rows
            rows = slice(first, first + block_rows)
            if b // blocks == 1:
                okb = row < jnp.where(listed, co_ref[inner], 0)
            else:
                mark = xs_ref[rows, 0:128].astype(F32)[:, 0:1]
                okb = jnp.broadcast_to(mark, (block_rows, block_rows)) < jnp.where(listed, 0.5 * ABSENT, -ABSENT)
            bias_s[rows, i * block_rows:(i + 1) * block_rows] = jnp.where(okb, 0.0, NEG_FILL)


def attend(ok, score_scale, bias_s, key_s, val_s, q_ref, g_ref, s_s, dw_s, wt_s, ds_s, emit):
    n, keys = q_ref.shape[0], key_s.shape[0]
    step = 64
    for c in range(0, q_ref.shape[1], 128):
        k_pair, v_pair = key_s[:, c:c + 128], val_s[:, c:c + 128]
        q_pair = q_ref[:, c:c + 128]
        g_pair = jnp.where(ok, g_ref[:, c:c + 128], jnp.zeros((n, 128), BF))
        k_t, v_t = k_pair.T, v_pair.T
        masked = [(lane_half(q_pair, half), lane_half(g_pair, half)) for half in range(2)]
        for half, (qm, gm) in enumerate(masked):
            s_s[half] = nt(k_pair, qm) + bias_s[...]
            dw_s[half] = nt(v_pair, gm)
        dk = dv = None
        out_t, dq_t = [], []
        for half, (qm, gm) in enumerate(masked):
            peak = jnp.full((8, n), NEG_FILL, F32)
            for r in range(0, keys, step):
                peak = jnp.maximum(peak, jnp.max(s_s[half, r:r + step, :].reshape(step // 8, 8, n), axis=0))
            peak = jnp.max(peak, axis=0, keepdims=True)
            total8 = delta8 = jnp.zeros((8, n), F32)
            for r in range(0, keys, step):
                e = jnp.exp(s_s[half, r:r + step, :] - peak)
                s_s[half, r:r + step, :] = e
                total8 = total8 + jnp.sum(e.reshape(step // 8, 8, n), axis=0)
                delta8 = delta8 + jnp.sum((e * dw_s[half, r:r + step, :]).reshape(step // 8, 8, n), axis=0)
            inv = 1.0 / jnp.sum(total8, axis=0, keepdims=True)
            delta = jnp.sum(delta8, axis=0, keepdims=True) * inv
            for r in range(0, keys, step):
                a = s_s[half, r:r + step, :] * inv
                wt_s[half, r:r + step, :] = a.astype(BF)
                ds_s[half, r:r + step, :] = (a * (dw_s[half, r:r + step, :] - delta)).astype(BF)
            wt, ds = wt_s[half], ds_s[half]
            out_t.append(nn(v_t[half * 64:half * 64 + 64], wt))
            dq_t.append(nn(k_t[half * 64:half * 64 + 64], ds))
            dk_half, dv_half = nn(ds, qm), nn(wt, gm)
            dk = dk_half if dk is None else dk + dk_half
            dv = dv_half if dv is None else dv + dv_half
        dq = (jnp.concatenate(dq_t, axis=0) * score_scale).astype(BF).T
        mixture = jnp.concatenate(out_t, axis=0).astype(BF).T
        emit(c, dk, dv, dq, jnp.where(ok, mixture, jnp.zeros((n, 128), BF)))


def low_kernel(blocks, block_rows, score_scale, pat_h, co_h, xl_h, xr_h, w_h, q_h, k_h, v_h, g_h, virt_h,
               out_h, dq_h, dkn_h, dvn_h, dko_h, dvo_h,
               xs_ref, w_ref, q_ref, g_ref, key_s, val_s, bias_s, s_s, dw_s, wt_s, ds_s,
               out_s, dq_s, dkn_s, dvn_s, dko_s, dvo_s, pat_ref, co_ref, sems):
    n, part = q_ref.shape
    cols = pl.ds(0, part)
    own, last = pl.ds(2 * n, n), pl.ds(3 * n, virt_h.shape[1])
    ready = loader((xl_h, xr_h, pat_h, co_h, w_h.at[1, :, cols], w_h.at[2, :, cols],
                    k_h.at[:, cols], v_h.at[:, cols], virt_h.at[1, :, cols], virt_h.at[2, :, cols],
                    q_h.at[:, cols], g_h.at[:, cols]),
                   (xs_ref.at[pl.ds(0, n)], xs_ref.at[pl.ds(n, n)], pat_ref, co_ref, w_ref.at[0], w_ref.at[1],
                    key_s.at[own], val_s.at[own], key_s.at[last], val_s.at[last], q_ref, g_ref), sems)
    out = Writer(sems, 12)
    ready(0, 1, 2, 3)
    fill_bias(blocks, block_rows, pat_ref, co_ref, xs_ref, bias_s)
    ready(4, 5)
    key_s[0:2 * n, :] = nn(xs_ref[...], w_ref[0]).astype(BF)
    val_s[0:2 * n, :] = nn(xs_ref[...], w_ref[1]).astype(BF)
    ready(6, 7, 8, 9, 10, 11)
    ok = own_row_ok(co_ref, blocks, block_rows, (n, 128))

    def emit(c, dk, dv, dq, mixture):
        here = pl.ds(c, 128)
        for value, ref, dst in ((dk[0:2 * n].astype(BF), dkn_s, dkn_h), (dv[0:2 * n].astype(BF), dvn_s, dvn_h),
                                (dk[2 * n:], dko_s, dko_h), (dv[2 * n:], dvo_s, dvo_h),
                                (dq, dq_s, dq_h), (mixture, out_s, out_h)):
            ref[:, c:c + 128] = value
            out.send(ref.at[:, here], dst.at[:, here])

    attend(ok, score_scale, bias_s, key_s, val_s, q_ref, g_ref, s_s, dw_s, wt_s, ds_s, emit)
    out.finish()


def high_kernel(blocks, block_rows, score_scale, pat_h, co_h, xl_h, xr_h, x_h, w_h, q_h, k_h, v_h, g_h, virt_h,
                vs_h, vcot_h, stats_h, dq_low_h, dkn_low_h, dvn_low_h, dko_low_h, dvo_low_h, out_low_h,
                out_h, send_h, keep_h, dq_h, dk_h, dv_h,
                xs_ref, w_ref, q_ref, g_ref, k_ref, v_ref, virt_ref, vcot_ref, stats_ref,
                key_s, val_s, bias_s, s_s, dw_s, wt_s, ds_s,
                out_s, dko_s, dvo_s, xt_s, dqw_s, dkw_s, dvw_s, pack_s, pat_ref, co_ref, sems):
    n, width = x_h.shape
    part = q_ref.shape[1]
    virtual_rows = vs_h.shape[0]
    low, high = pl.ds(0, width - part), pl.ds(width - part, part)
    near, own, last = pl.ds(0, 2 * n), pl.ds(2 * n, n), pl.ds(3 * n, virtual_rows)
    first = pl.ds(0, n)
    ready = loader((xl_h, xr_h, pat_h, co_h, w_h.at[1], w_h.at[2],
                    k_h.at[:, high], v_h.at[:, high], virt_h.at[1, :, high], virt_h.at[2, :, high],
                    q_h.at[:, high], g_h.at[:, high],
                    x_h, vs_h, w_h.at[0], k_h, v_h, virt_h.at[0], vcot_h, stats_h,
                    dq_low_h, dkn_low_h, dvn_low_h, dko_low_h, dvo_low_h),
                   (xs_ref.at[pl.ds(0, n)], xs_ref.at[pl.ds(n, n)], pat_ref, co_ref, w_ref.at[1], w_ref.at[2],
                    key_s.at[own], val_s.at[own], key_s.at[last], val_s.at[last], q_ref, g_ref,
                    xs_ref.at[own], xs_ref.at[last], w_ref.at[0], k_ref, v_ref, virt_ref, vcot_ref, stats_ref,
                    dqw_s.at[first, low], dkw_s.at[near, low], dvw_s.at[near, low], dko_s.at[:, low], dvo_s.at[:, low]),
                   sems)
    out = Writer(sems, 25)
    ready(0, 1, 2, 3)
    fill_bias(blocks, block_rows, pat_ref, co_ref, xs_ref, bias_s)
    ready(4, 5)
    key_s[0:2 * n, :] = nn(xs_ref[0:2 * n, :], w_ref[1, :, width - part:]).astype(BF)
    val_s[0:2 * n, :] = nn(xs_ref[0:2 * n, :], w_ref[2, :, width - part:]).astype(BF)
    ready(6, 7, 8, 9, 10, 11, 12, 13)
    ok = own_row_ok(co_ref, blocks, block_rows, (n, 128))
    for c in range(0, width, 128):
        xt_s[c:c + 128, :] = xs_ref[:, c:c + 128].T

    def emit(c, dk, dv, dq, mixture):
        here = slice(width - part + c, width - part + c + 128)
        dkw_s[0:2 * n, here] = dk[0:2 * n].astype(BF)
        dvw_s[0:2 * n, here] = dv[0:2 * n].astype(BF)
        dko_s[:, here] = dk[2 * n:]
        dvo_s[:, here] = dv[2 * n:]
        dqw_s[0:n, here] = dq
        out_s[:, c:c + 128] = mixture
        out.send(out_s.at[:, pl.ds(c, 128)], out_h.at[:, pl.ds(width - part + c, 128)])

    attend(ok, score_scale, bias_s, key_s, val_s, q_ref, g_ref, s_s, dw_s, wt_s, ds_s, emit)
    ready(*range(14, 25))
    out.send(dkw_s.at[near], dk_h.at[near])
    out.send(dvw_s.at[near], dv_h.at[near])
    out.send(dqw_s.at[first], dq_h)
    pairs = width // 128
    stats = stats_ref[...]
    peak = jnp.max(stats[:, 0:pairs], axis=0)
    factor = jnp.exp(stats[:, 0:pairs] - peak[None])
    total = jnp.sum(stats[:, pairs:2 * pairs] * factor, axis=0)
    delta = jnp.sum(stats[:, 2 * pairs:3 * pairs] * factor, axis=0) / total
    inv_total = 1.0 / total
    lane_low = lax.broadcasted_iota(jnp.int32, (virtual_rows, 128), 1) < 64

    def diagonal(square):
        return jnp.where(lane_low, square[:virtual_rows], square[virtual_rows:])

    mixed = []
    for p in range(pairs):
        c = p * 128
        k_pair, v_pair = k_ref[:, c:c + 128], v_ref[:, c:c + 128]
        vq = both_heads(virt_ref[:, c:c + 128])
        vcot = both_heads(vcot_ref[:, c:c + 128])
        scores = jnp.where(ok, nt(k_pair, vq * score_scale), NEG_FILL)
        attn = jnp.exp(scores - peak[p:p + 1]) * inv_total[p:p + 1]
        attn_bf = attn.astype(BF)
        dw = nt(v_pair, vcot)
        ds = (attn * (dw - delta[p:p + 1]) * score_scale).astype(BF)
        mixed.append(diagonal(tn(attn_bf, v_pair)))
        dqw_s[n:n + virtual_rows, c:c + 128] = diagonal(tn(ds, k_pair)).astype(BF)
        dkw_s[2 * n:3 * n, c:c + 128] = (dko_s[0:n, c:c + 128] + nn(ds, vq)).astype(BF)
        dvw_s[2 * n:3 * n, c:c + 128] = (dvo_s[0:n, c:c + 128] + nn(attn_bf, vcot)).astype(BF)
    dkw_s[3 * n:3 * n + virtual_rows, :] = dko_s[n:n + virtual_rows, :].astype(BF)
    dvw_s[3 * n:3 * n + virtual_rows, :] = dvo_s[n:n + virtual_rows, :].astype(BF)
    out.send(dkw_s.at[own], dk_h.at[own])
    out.send(dvw_s.at[own], dv_h.at[own])
    me = place()
    row_groups = width // 64
    for c in range(0, width, 256):
        for t in range(3):
            if t == 0:
                wg = nn(xt_s[:, 2 * n:], dqw_s[:, c:c + 256])
            else:
                wg = nn(xt_s[...], (dkw_s if t == 1 else dvw_s)[:, c:c + 256])
            for col in range(0, 256, 128):
                for group in range(row_groups):
                    at = jnp.bitwise_xor(me, (c + col) // 128 * row_groups + group)
                    pack_s[at, t * 64:(t + 1) * 64, :] = wg[group * 64:(group + 1) * 64, col:col + 128].astype(BF)
    vg = (nt(dqw_s[n:n + virtual_rows, :], w_ref[0]) + nt(dkw_s[3 * n:3 * n + virtual_rows, :], w_ref[1])
          + nt(dvw_s[3 * n:3 * n + virtual_rows, :], w_ref[2]))
    for p in range(pairs):
        for group in range(row_groups):
            at = jnp.bitwise_xor(me, p * row_groups + group)
            rows = slice(group * 8, group * 8 + 8)
            pack_s[at, 192:208, :] = jnp.concatenate(
                [vg[rows, p * 128:(p + 1) * 128], mixed[p][rows]], axis=0).astype(BF)
    out.send(pack_s.at[pl.ds(SHARDS // 2, SHARDS // 2)], send_h)
    out.send(pack_s.at[pl.ds(0, SHARDS // 2)], keep_h)
    out.finish()


def node_kernel(w_h, dq_h, dk_h, dv_h, left_h, right_h, part_h, w_ref, dq_ref, dk_ref, dv_ref,
                left_s, right_s, part_s, sems):
    n = dq_ref.shape[0]
    ready = loader((w_h, dq_h, dk_h, dv_h), (w_ref, dq_ref, dk_ref, dv_ref), sems)
    out = Writer(sems, 4)
    ready(0, 1, 2, 3)
    for at, ref, dst in ((0, left_s, left_h), (1, right_s, right_h), (2, part_s, part_h)):
        rows = slice(at * n, (at + 1) * n)
        grad = nt(dk_ref[rows, :], w_ref[1]) + nt(dv_ref[rows, :], w_ref[2])
        if at == 2:
            grad = grad + nt(dq_ref[...], w_ref[0])
        ref[...] = grad.astype(ref.dtype)
        out.send(ref, dst)
    out.finish()


def unpack_kernel(second, part_h, *refs):
    wg_h, vg_h, vo_h, part_ref, wg_s, vg_s, vo_s, vgb_s, vob_s, sems = refs[3 * second:]
    row_groups = wg_s.shape[1] // 64
    ready = loader((part_h,), (part_ref,), sems)
    out = Writer(sems, 1)
    me = jnp.bitwise_and(place(), SHARDS // 2 - 1)
    core = jnp.bitwise_and(lax.axis_index("dp"), 1)
    if second:
        core = 1 - core
    half = wg_s.shape[2]
    columns = pl.ds(pl.multiple_of(core * half, half), half)
    ready(0)
    for t in range(3):
        for p in range(SHARDS // 2):
            shard = jnp.bitwise_xor(me, p)
            cols = pl.ds(pl.multiple_of((shard // row_groups) * 128, 128), 128)
            group = lax.rem(shard, row_groups)
            rows = pl.ds(pl.multiple_of(group * 64, 64), 64)
            wg_s[t, rows, cols] = part_ref[p, t * 64:(t + 1) * 64, :].astype(F32)
            if t == 0:
                rows = pl.ds(pl.multiple_of(group * 8, 8), 8)
                both = part_ref[p, 192:208, :].astype(F32)
                vg_s[rows, cols] = both[0:8]
                vo_s[rows, cols] = both[8:16]
        out.send(wg_s.at[t], wg_h.at[t, :, columns])
    vgb_s[...] = vg_s[...].astype(BF)
    vob_s[...] = vo_s[...].astype(BF)
    out.send(vgb_s, vg_h.at[:, columns])
    out.send(vob_s, vo_h.at[:, columns])
    out.finish()


ANY = pl.BlockSpec(memory_space=pl.ANY)


def call(body, args, outs, scratch, sems, flops=1e8, name=None, vmem=VMEM_BYTES, aliases=None):
    return pl.pallas_call(
        body,
        out_shape=[jax.ShapeDtypeStruct(s, d) for s, d in outs],
        in_specs=[ANY] * len(args),
        out_specs=[ANY] * len(outs),
        scratch_shapes=[pltpu.SMEM(s, d) if d == jnp.int32 else pltpu.VMEM(s, d) for s, d in scratch] + [pltpu.SemaphoreType.DMA((sems,))],
        compiler_params=pltpu.CompilerParams(vmem_limit_bytes=vmem),
        cost_estimate=pl.CostEstimate(flops=int(flops), bytes_accessed=4 << 20, transcendentals=0),
        input_output_aliases=aliases or {},
        name=name,
    )(*args)


def ring(value, steps):
    count = lax.axis_size("loop")
    return lax.ppermute(value, "loop", [(s, (s + steps) % count) for s in range(count)])


def swap(value, loop_bits, lane_bits):
    lanes = lax.axis_size("dp")
    count = lax.axis_size("loop") * lanes
    other = loop_bits * lanes + lane_bits
    return lax.ppermute(value, ("loop", "dp"), [(s, s ^ other) for s in range(count)])


def together(tree):
    return lax.optimization_barrier(tree)


PLANE = ((3, 1, 2), (1, 1, 0), (2, 0, 2))
LINE = ((3, 6, 0), (2, 4, 0), (1, 2, 0))


def scatter(held, links):
    rows = held.shape[0] // 4
    return [swap(held[at * rows:(at + 1) * rows], *bits) for at, *bits in links]


def gather(held, links):
    return [swap(held, *bits) for _, *bits in links]


def in_order(held, got, links):
    parts = dict(zip([at for at, *_ in links], got))
    return jnp.concatenate([held] + [parts[at] for at in (1, 2, 3)], axis=0)


def total(parts):
    summed = parts[0].astype(F32)
    for part in parts[1:]:
        summed = summed + part.astype(F32)
    return summed.astype(BF)


def reduce_all(keep, send, own_part, to_left, to_right):
    loop_size = lax.axis_size("loop")
    held = total([keep, swap(send, 0, 1)])
    held = together(held)
    got, own_part, to_left, to_right = together((scatter(held, PLANE), own_part, to_left, to_right))
    held, to_left, to_right = together((total([held[:held.shape[0] // 4]] + got), to_left, to_right))
    from_right, from_left = ring(to_left, -1), ring(to_right, 1)
    got = together(scatter(held, LINE))
    piece = total([held[:1]] + got)
    bit = 8
    while bit < loop_size:
        piece = total([piece, swap(piece, bit, 0)])
        bit *= 2
    piece = together(piece)
    got, from_right, from_left = together((gather(piece, LINE), from_right, from_left))
    held = together(in_order(piece, got, LINE))
    got, node_grad = together((gather(held, PLANE), total([own_part, from_right, from_left])))
    held = together(in_order(held, got, PLANE))
    return held, swap(held, 0, 1), node_grad


def local(node_states, virtual_states, projection, pattern, valid_counts, node_cotangent, virtual_cotangent):
    n, width = node_states.shape
    blocks = pattern.shape[0]
    block_rows = n // blocks
    virtual_rows = virtual_states.shape[0]
    loop_size, lanes = lax.axis_size("loop"), lax.axis_size("dp")
    devices = loop_size * lanes
    score_scale = (width // H) ** -0.5
    keys = 3 * n + virtual_rows

    shape = (blocks, block_rows, width)
    place_in_block = lax.broadcasted_iota(jnp.int32, shape, 1) * width + lax.broadcasted_iota(jnp.int32, shape, 2)
    valid = place_in_block < lax.broadcast_in_dim(valid_counts * width, shape, (0,))
    marked = jnp.where(valid, node_states.reshape(shape), jnp.asarray(ABSENT, BF)).reshape(n, width)
    x_left, x_right = ring(marked, 1), ring(marked, -1)

    counts_i, pattern_i = ((blocks,), jnp.int32), (pattern.shape, jnp.int32)
    rows_bf, rows_f = ((n, width), BF), ((n, width), F32)
    wide = ((3, width, width), BF)
    virt_bf, virt_f = ((virtual_rows, width), BF), ((virtual_rows, width), F32)
    triple = ((3, virtual_rows, width), BF)
    stats_f = ((devices, 16, 128), F32)
    q, k, v, virt, stats = call(
        functools.partial(project_kernel, blocks, block_rows, score_scale),
        (valid_counts, node_states, projection, virtual_states, virtual_cotangent),
        [rows_bf] * 3 + [triple, stats_f],
        [rows_bf, wide, virt_bf, virt_bf] + [rows_bf] * 3 + [triple, stats_f, counts_i], 12, name="project")
    stats = lax.all_to_all(stats, ("loop", "dp"), 0, 0, tiled=True)

    part, rest = width // 4 * 3, width // 4
    keys_bf, keys_part, keys_rest = ((keys, width), BF), ((keys, part), BF), ((keys, rest), BF)
    rows_rest = ((n, rest), BF)
    rows_part, near_part, mine_part = ((n, part), BF), ((2 * n, part), BF), ((n + virtual_rows, part), F32)
    mine_f = ((n + virtual_rows, width), F32)
    passes = [((keys, n), F32)] + [((2, keys, n), F32)] * 2 + [((2, keys, n), BF)] * 2
    window = (pattern, valid_counts, x_left, x_right)
    half_out, *low = call(
        functools.partial(low_kernel, blocks, block_rows, score_scale),
        (*window, projection, q, k, v, node_cotangent, virt),
        [rows_bf, rows_part, near_part, near_part, mine_part, mine_part],
        [((2 * n, width), BF), ((2, width, part), BF), rows_part, rows_part, keys_part, keys_part] + passes
        + [rows_part, rows_part, near_part, near_part, mine_part, mine_part, pattern_i, counts_i], 30,
        flops=1e10, name="attention_low")
    half = ((SHARDS // 2, 3 * 64 + 16, 128), BF)
    window_bf = ((3 * n, width), BF)
    node_out, send, keep, dq, dk, dv = call(
        functools.partial(high_kernel, blocks, block_rows, score_scale),
        (*window, node_states, projection, q, k, v, node_cotangent, virt, virtual_states, virtual_cotangent, stats, *low,
         half_out),
        [rows_bf, half, half, rows_bf, window_bf, window_bf],
        [keys_bf, wide, rows_rest, rows_rest, rows_bf, rows_bf, virt_bf, virt_bf, stats_f, keys_rest, keys_rest] + passes
        + [rows_rest, mine_f, mine_f, ((width, keys), BF), ((n + virtual_rows, width), BF), keys_bf, keys_bf,
           ((SHARDS, 3 * 64 + 16, 128), BF), pattern_i, counts_i], 36,
        flops=1e10, name="attention_high", aliases={19: 0})
    to_left, to_right, own_part = call(
        node_kernel, (projection, dq, dk, dv), [rows_bf, rows_bf, rows_f],
        [wide, rows_bf, window_bf, window_bf, rows_bf, rows_bf, rows_f], 7, flops=1e9, name="node_grads")
    mine, other, node_grad = reduce_all(keep, send, own_part, to_left, to_right)
    halves_f = ((virtual_rows, width // 2), F32)
    unpack = functools.partial(
        call, outs=[((3, width, width), F32), virt_bf, virt_bf],
        scratch=[half, ((3, width, width // 2), F32), halves_f, halves_f] + [((virtual_rows, width // 2), BF)] * 2, sems=6,
        vmem=16 << 20)
    results = unpack(functools.partial(unpack_kernel, 0), (mine,), name="unpack_mine")
    weight_grads, virtual_grad, virtual_out = unpack(
        functools.partial(unpack_kernel, 1), (other, *results), name="unpack_other", aliases={1: 0, 2: 1, 3: 2})
    return node_out, virtual_out, node_grad, virtual_grad, weight_grads


def solution(mesh):
    return jax.shard_map(
        local,
        mesh=mesh,
        in_specs=(
            P(("loop", "dp"), None),
            P(),
            P(),
            P(("loop", "dp"), None),
            P(("loop", "dp")),
            P(("loop", "dp"), None),
            P(),
        ),
        out_specs=(P(("loop", "dp"), None), P(), P(("loop", "dp"), None), P(), P()),
        check_vma=False,
    )
```
